32 devices in a mesh: seq: 4 (over x, core), head: 8 (over z, y).
Axes of the slice: x: 2, y: 2, z: 4, core: 2. Of those that a mesh axis runs over, the one named last changes fastest.
Arguments:
- queries: float32 [1024, 512], P('seq', 'head'), may hold values from -50 to 50
- keys: float32 [1024, 512], P('seq', 'head'), may hold values from -16 to 16
- values: float32 [1024, 512], P('seq', 'head'), may hold values from -6 to 6
- local_span: int32 [4], replicated, may hold values from 1 to 2
- wo_local: float32 [512, 4096], P('head'), may hold values from -0.25 to 0.25
- wo_strided: float32 [512, 4096], P('head'), may hold values from -0.25 to 0.25
- grad_out: bfloat16 [1024, 4096], P('seq', 'head'), may hold values from -6 to 6
Outputs:
- mixed: float32 [1024, 4096], P('seq', 'head')
- grad_queries: float32 [1024, 512], P('seq', 'head')
- grad_keys: float32 [1024, 512], P('seq', 'head')
- grad_values: float32 [1024, 512], P('seq', 'head')
The draws below stay inside these ranges and needn't reach their ends.
All inputs are finite; a program needn't handle non-finite values.
Results may differ from the reference program's by a relative error of at most 0.0003.
Values may be sent and summed in bfloat16 or wider, within the bound.
A program may use at most 64 MiB of HBM per device.

```python
import jax
import jax.numpy as jnp
from jax import lax

D = 4096
HDIM = 128
BLOCK = 128
GROUP_BLK = 2
STRIDE = 128
TOKENS = 1024
HEADS = 4


def query_key_pair(key):
    base = jax.random.fold_in(key, 7)
    key_q, key_k = jax.random.split(base, 2)
    layout = (TOKENS, HEADS, HDIM)
    query_all = jnp.clip(jax.random.normal(key_q, layout, jnp.float32), -6.0, 6.0)
    key_all = jnp.clip(jax.random.normal(key_k, layout, jnp.float32), -6.0, 6.0)
    return (query_all.reshape(TOKENS, HEADS * HDIM), key_all.reshape(TOKENS, HEADS * HDIM))


def draw_queries(key, part):
    return query_key_pair(key)[0]


def draw_keys(key, part):
    return query_key_pair(key)[1]


def draw_local_span(key, part):
    key_one, key_two = jax.random.split(jax.random.fold_in(key, 11))
    spans = jax.random.randint(key_one, (HEADS,), 1, GROUP_BLK + 1)
    picked = jax.random.randint(key_two, (), 0, HEADS)
    return jnp.where(jnp.arange(HEADS) == picked, GROUP_BLK, spans).astype(jnp.int32)


def spiked(drawn, own_key, source, target, parts, factor):
    owner, partner = [(jnp.arange(drawn.shape[axis_at]) // (drawn.shape[axis_at] // parts)).reshape([-1 if axis == axis_at else 1 for axis in range(drawn.ndim)]) for axis_at in (source, target)]
    chosen = jax.random.permutation(own_key, parts)[partner]
    strong = (owner == chosen) | (owner == (partner + parts // 2) % parts)
    return jnp.where(strong, factor * drawn, drawn)


def shard_levels(key, dims, shards, smallest, high):
    def one(dim, parts):
        heights = jax.random.uniform(jax.random.fold_in(jax.random.fold_in(key, 6), dim), (parts,), jnp.float32, smallest / len(shards), high / len(shards))
        return jnp.repeat(jnp.exp(heights), dims[dim] // parts).reshape((-1,) + (1,) * (len(dims) - dim - 1))

    factor_of = one(*shards[0])
    for cut in shards[1:]:
        factor_of = factor_of * one(*cut)
    return factor_of


def noise(rng, shape, deviation, most, cuts=(), held_as=jnp.bfloat16):
    level = shard_levels(rng, shape, cuts, -0.22, 0.18) if cuts else 1.0
    result = jax.random.normal(rng, shape, jnp.float32) * deviation * level
    return jnp.minimum(jnp.maximum(result, -most), most).astype(held_as)


def bell_draw_with(rng, shape, spread, limit, cuts, heavy, held_as=jnp.bfloat16):
    entries = spread * jax.random.normal(rng, shape, jnp.float32)
    if cuts:
        entries = entries * shard_levels(rng, shape, cuts, -0.22, 0.18)
    return jnp.clip(spiked(entries, jax.random.fold_in(rng, 3), *heavy), -limit, limit).astype(held_as)


def setup_inputs(seed: int = 0) -> dict:
    arg_keys = jax.random.split(jax.random.key(seed), 8)
    queries = draw_queries(jax.random.fold_in(arg_keys[7], 71), 0)
    keys = draw_keys(jax.random.fold_in(arg_keys[7], 71), 0)
    values = noise(arg_keys[2], (TOKENS, HEADS * HDIM), 1.0, 6.0, ((0, 4), (1, 8)), jnp.float32)
    local_span = draw_local_span(jax.random.fold_in(arg_keys[7], 71), 0)
    wo_local = bell_draw_with(arg_keys[4], (HEADS * HDIM, D), (2 * HEADS * HDIM) ** -0.5, 0.25, ((0, 8),), (0, 1, 8, 2.0), jnp.float32)
    wo_strided = bell_draw_with(arg_keys[5], (HEADS * HDIM, D), (2 * HEADS * HDIM) ** -0.5, 0.25, ((0, 8),), (0, 1, 8, 2.0), jnp.float32)
    grad_out = noise(arg_keys[6], (TOKENS, D), 1.0, 6.0, ((0, 4), (1, 8)))
    return {"queries": queries, "keys": keys, "values": values, "local_span": local_span, "wo_local": wo_local, "wo_strided": wo_strided, "grad_out": grad_out}


HIGHEST = lax.Precision.HIGHEST


def attend_forward(query_part, key_part, value_part, allowed):
    scale_factor = HDIM ** -0.5
    scores = jnp.einsum("bqhd,bkhd->bhqk", query_part, key_part, precision=HIGHEST) * scale_factor
    row_max = jnp.max(jnp.where(allowed, scores, -jnp.inf), axis=-1, keepdims=True)
    weights = jnp.where(allowed, jnp.exp(scores - row_max), 0.0)
    probs = weights / jnp.sum(weights, axis=-1, keepdims=True)
    attended = jnp.einsum("bhqk,bkhd->bqhd", probs, value_part, precision=HIGHEST)
    return attended, probs


def attend_backward(query_part, key_part, value_part, probs, attended, incoming):
    scale_factor = HDIM ** -0.5
    dprobs = jnp.einsum("bqhd,bkhd->bhqk", incoming, value_part, precision=HIGHEST)
    row_delta = jnp.transpose(jnp.sum(incoming * attended, axis=-1), (0, 2, 1))[..., None]
    dscores = probs * (dprobs - row_delta)
    grad_query = jnp.einsum("bhqk,bkhd->bqhd", dscores, key_part, precision=HIGHEST) * scale_factor
    grad_key = jnp.einsum("bhqk,bqhd->bkhd", dscores, query_part, precision=HIGHEST) * scale_factor
    grad_value = jnp.einsum("bhqk,bqhd->bkhd", probs, incoming, precision=HIGHEST)
    return grad_query, grad_key, grad_value


def reference(queries, keys, values, local_span, wo_local, wo_strided, grad_out):
    group_len = GROUP_BLK * BLOCK
    groups = TOKENS // group_len
    runs = TOKENS // STRIDE
    local_layout = (groups, group_len, HEADS, HDIM)
    local_q = queries.reshape(local_layout)
    local_k = keys.reshape(local_layout)
    local_v = values.reshape(local_layout)
    position = jnp.arange(group_len)
    block_of = position // BLOCK
    causal = position[None, None, :] <= position[None, :, None]
    reach = (block_of[None, :, None] - block_of[None, None, :]) < local_span[:, None, None]
    allowed_local = (causal & reach)[None]

    def to_runs(matrix):
        return matrix.reshape(runs, STRIDE, HEADS, HDIM).transpose(1, 0, 2, 3)

    def from_runs(stacked):
        return stacked.transpose(1, 0, 2, 3).reshape(TOKENS, HEADS * HDIM)

    strided_q = to_runs(queries)
    strided_k = to_runs(keys)
    strided_v = to_runs(values)
    order = jnp.arange(runs)
    allowed_strided = (order[None, :] <= order[:, None])[None, None]

    attn_local, probs_local = attend_forward(local_q, local_k, local_v, allowed_local)
    attn_strided, probs_strided = attend_forward(strided_q, strided_k, strided_v, allowed_strided)
    flat_local = attn_local.reshape(TOKENS, HEADS * HDIM)
    flat_strided = from_runs(attn_strided)
    mixed = jnp.dot(flat_local, wo_local, precision=HIGHEST, preferred_element_type=jnp.float32)
    mixed = mixed + jnp.dot(flat_strided, wo_strided, precision=HIGHEST, preferred_element_type=jnp.float32)

    grad_all = grad_out.astype(jnp.float32)
    grad_local = jnp.dot(grad_all, wo_local.T, precision=HIGHEST, preferred_element_type=jnp.float32)
    grad_strided = jnp.dot(grad_all, wo_strided.T, precision=HIGHEST, preferred_element_type=jnp.float32)
    dq_local, dk_local, dv_local = attend_backward(local_q, local_k, local_v, probs_local, attn_local, grad_local.reshape(local_layout))
    dq_strided, dk_strided, dv_strided = attend_backward(strided_q, strided_k, strided_v, probs_strided, attn_strided, to_runs(grad_strided))
    grad_queries = dq_local.reshape(TOKENS, HEADS * HDIM) + from_runs(dq_strided)
    grad_keys = dk_local.reshape(TOKENS, HEADS * HDIM) + from_runs(dk_strided)
    grad_values = dv_local.reshape(TOKENS, HEADS * HDIM) + from_runs(dv_strided)
    return (mixed, grad_queries, grad_keys, grad_values)
```

```python
import functools

import jax
import jax.numpy as jnp
from jax import lax
from jax.experimental import pallas as pl
from jax.experimental.pallas import tpu as pltpu
from jax.sharding import PartitionSpec as P

HDIM = 128
STRIDE = 128
HALF = HDIM // 2
RUNS = 2
HIGHEST = lax.Precision.HIGHEST
NN = (((1,), (0,)), ((), ()))
NT = (((1,), (1,)), ((), ()))
TN = (((0,), (0,)), ((), ()))


def exact_dot(a, b, dims):
    return lax.dot_general(a, b, dims, precision=HIGHEST, preferred_element_type=jnp.float32)


def bf16_dot(a, b, dims):
    return lax.dot_general(a, b, dims, preferred_element_type=jnp.float32)


def halves(x):
    high = x.astype(jnp.bfloat16)
    return high, (x - high.astype(jnp.float32)).astype(jnp.bfloat16)


def split_dot(a, b, dims):
    (a_high, a_low), (b_high, b_low) = halves(a), halves(b)
    return bf16_dot(a_high, b_high, dims) + (
        bf16_dot(a_high, b_low, dims) + bf16_dot(a_low, b_high, dims)
    )


def kernel(
    seqs, heads, share,
    span_ref, pack_ref, gout_ref, wo_local_ref, wo_strided_ref,
    mixed_ref, grads_ref,
    w_buf, pack_buf, gout_buf, q_buf, k_buf, v_buf, p_buf, attn_own, attn_buf,
    gpart, g_buf, m_buf, m_recv, e_out, e_buf,
    w_send, w_recv, share_send, pack_send, pack_recv, gout_send, gout_recv,
    attn_send, attn_recv, g_send, g_recv, m_send, m_recv_sem, e_send, e_recv,
):
    pairs = heads // 2
    res = STRIDE // seqs
    piece = RUNS * res
    rows = seqs * piece
    w_rows = HALF // share
    width = gout_ref.shape[1]
    me_s = lax.axis_index("seq")
    me_h = lax.axis_index("head")
    pair = lax.div(me_h, 2)
    side = lax.rem(me_h, 2)
    partner = me_h + 1 - 2 * side
    quarter = lax.rem(me_s, share)

    def to_seq(t):
        return (1 - side) * me_s + side * t

    def to_slot(t):
        return (1 - side) * t + side * me_s

    def flip(value, distance):
        return value + distance - 2 * distance * lax.rem(lax.div(value, distance), 2)

    def is_me(s, h):
        return jnp.logical_and(s == me_s, h == me_h)

    def remote(src, dst, send_sem, recv_sem, s, h):
        return pltpu.make_async_remote_copy(
            src_ref=src, dst_ref=dst, send_sem=send_sem, recv_sem=recv_sem,
            device_id=(s, h), device_id_type=pl.DeviceIdType.MESH,
        )

    def send(src, dst, send_sem, recv_sem, s, h):
        same = is_me(s, h)

        @pl.when(same)
        def _():
            pltpu.make_async_copy(src, dst, recv_sem).start()

        @pl.when(jnp.logical_not(same))
        def _():
            remote(src, dst, send_sem, recv_sem, s, h).start()

    def sent(src, dst, send_sem, recv_sem, s, h):
        @pl.when(jnp.logical_not(is_me(s, h)))
        def _():
            remote(src, dst, send_sem, recv_sem, s, h).wait_send()

    def arrived(dst, recv_sem):
        pltpu.make_async_copy(dst, dst, recv_sem).wait()

    def loop(count, body):
        def step(i, carry):
            body(i)
            return carry
        lax.fori_loop(0, count, step, 0)

    barrier = pltpu.get_barrier_semaphore()

    def greet(i):
        s, h = lax.div(i, heads), lax.rem(i, heads)
        near = jnp.logical_or(s == me_s, lax.div(h, 2) == pair)
        odd = jnp.logical_and(lax.rem(h, 2) == 1, side == 1)
        wanted = jnp.logical_or(near, odd)

        @pl.when(jnp.logical_and(wanted, jnp.logical_not(is_me(s, h))))
        def _():
            pl.semaphore_signal(
                barrier, inc=1, device_id=(s, h), device_id_type=pl.DeviceIdType.MESH
            )

    loop(seqs * heads, greet)
    pl.semaphore_wait(
        barrier, heads - 1 + 2 * (seqs - 1) + side * (seqs - 1) * (pairs - 1)
    )

    def pack_copies(act, t):
        for other in range(2):
            s = (1 - other) * me_s + other * t
            slot = (1 - other) * t + other * me_s
            act(
                pack_ref.at[t], pack_buf.at[side, slot], pack_send.at[other, t],
                pack_recv.at[side, slot], s, 2 * pair + other,
            )

    loop(seqs, functools.partial(pack_copies, send))

    def w_copies(act, step):
        z = lax.rem(step + pair, pairs)
        own_rows = pl.ds(pl.multiple_of(quarter * w_rows, 8), w_rows)
        cols = pl.ds(pl.multiple_of(z * 2 * width, 128), 2 * width)
        for other, source in ((0, wo_local_ref), (1, wo_strided_ref)):
            act(
                source.at[own_rows, cols], w_buf.at[me_h, quarter], w_send.at[z, other],
                w_recv.at[me_h, quarter], me_s, 2 * z + other,
            )

    loop(pairs, functools.partial(w_copies, send))

    gout_copy = remote(
        gout_ref, gout_buf.at[side], gout_send.at[0], gout_recv.at[0], me_s, partner
    )
    gout_copy.start()
    gout_buf[side] = gout_ref[...]

    def share_copy(act, j, stage, offset_at, offset, distance):
        q = quarter
        for bit in (1, 2, 4, 8, 16, 32):
            if offset & bit:
                q = flip(q, bit)
        act(
            w_buf.at[j, q], w_buf.at[j, q], share_send.at[j, stage + offset_at],
            w_recv.at[j, q], flip(me_s, distance), me_h,
        )

    def w_arrived(j, offset):
        q = quarter
        for bit in (1, 2, 4, 8, 16, 32):
            if offset & bit:
                q = flip(q, bit)
        arrived(w_buf.at[j, q], w_recv.at[j, q])

    stages, held, fresh, distance = [], [0], [0], share // 2
    while distance:
        stages.append((distance, tuple(held), tuple(fresh)))
        fresh = [offset ^ distance for offset in held]
        held = held + fresh
        distance //= 2

    def run_stage(at):
        distance, held_here, fresh_here = stages[at]
        first = sum(len(s[1]) for s in stages[:at])

        def body(j):
            for n, offset in enumerate(held_here):
                if offset in fresh_here:
                    w_arrived(j, offset)
                share_copy(send, j, first, n, offset, distance)

        loop(heads, body)

    run_stage(0)

    for c in range(2):
        for t in range(seqs):
            arrived(pack_buf.at[c, t], pack_recv.at[c, t])

    lane = lax.broadcasted_iota(jnp.int32, (rows, HDIM), 1) < HALF
    lane_half = lax.broadcasted_iota(jnp.int32, (rows // 2, HDIM), 1) < HALF

    def turn(x):
        return pltpu.roll(x, HALF, 1)

    qk_first = pack_buf[0, :, :RUNS].reshape(rows, HDIM)
    qk_second = pack_buf[1, :, :RUNS].reshape(rows, HDIM)
    q_buf[...] = jnp.where(lane, qk_first, turn(qk_second))
    k_buf[...] = jnp.where(lane, turn(qk_first), qk_second)
    v_first = pack_buf[0, :, RUNS].reshape(rows // 2, HDIM)
    v_second = pack_buf[1, :, RUNS].reshape(rows // 2, HDIM)
    v_buf[:, 0] = jnp.where(lane_half, v_first, turn(v_second)).reshape(seqs, res, HDIM)
    v_buf[:, 1] = jnp.where(lane_half, turn(v_first), v_second).reshape(seqs, res, HDIM)

    res_bits = res.bit_length() - 1

    def place(dim):
        index = lax.broadcasted_iota(jnp.int32, (rows, rows), dim)
        run = (index >> res_bits) & 1
        part = index >> (res_bits + 1)
        residue = index & (res - 1)
        return run, part, residue

    run_i, part_i, residue_i = place(0)
    run_j, part_j, residue_j = place(1)
    at_i = run_i * STRIDE + part_i * res + residue_i
    at_j = run_j * STRIDE + part_j * res + residue_j
    local_ok = jnp.where((at_j <= at_i) & (run_i - run_j < span_ref[pair]), 1, 0)
    order_ok = RUNS * part_j + run_j <= RUNS * part_i + run_i
    strided_ok = jnp.where((residue_i == residue_j) & order_ok, 1, 0)
    allowed = local_ok * (1 - side) + strided_ok * side > 0

    scale = HDIM ** (-0.5)
    scores = exact_dot(q_buf[...], k_buf[...], NT) * scale
    row_max = jnp.max(jnp.where(allowed, scores, -jnp.inf), axis=-1, keepdims=True)
    weights = jnp.where(allowed, jnp.exp(scores - row_max), 0.0)
    probs = weights / jnp.sum(weights, axis=-1, keepdims=True)
    p_buf[...] = probs
    attended = exact_dot(probs, v_buf[...].reshape(rows, HDIM), NN)
    attn_own[...] = attended.reshape(seqs, piece, HDIM)

    def attn_copies(act, step):
        z = lax.rem(step + pair, pairs)

        def one(t):
            act(
                attn_own.at[t], attn_buf.at[pair, to_slot(t)], attn_send.at[z, t],
                attn_recv.at[pair, to_slot(t)], to_seq(t), 2 * z + side,
            )

        loop(seqs, one)

    loop(pairs, functools.partial(attn_copies, send))

    for at in range(1, len(stages)):
        run_stage(at)

    def last_of_w(j):
        for offset in fresh:
            w_arrived(j, offset)

    loop(heads, last_of_w)

    gout_copy.wait_recv()

    def head_rows(g):
        return w_buf[pl.ds(2 * g, 2)].reshape(HDIM, 2 * width)

    def g_copies(act, g):
        def one(t):
            act(
                gpart.at[g, t], g_buf.at[pair, to_slot(t)], g_send.at[g, t],
                g_recv.at[pair, to_slot(t)], to_seq(t), 2 * g + side,
            )

        loop(seqs, one)

    def partial_grad(step):
        g = lax.rem(step + pair, pairs)
        w_high, w_low = halves(head_rows(g))
        total = jnp.zeros((rows, HDIM), jnp.float32)
        for c in range(2):
            cols = slice(c * width, (c + 1) * width)
            out = gout_buf[c]
            total = total + (
                bf16_dot(out, w_high[:, cols], NT) + bf16_dot(out, w_low[:, cols], NT)
            )
        gpart[g] = total.reshape(seqs, piece, HDIM)
        g_copies(send, g)

    loop(pairs, partial_grad)

    m_buf[...] = jnp.zeros_like(m_buf)

    def partial_mixed(g):
        loop(seqs, lambda t: arrived(attn_buf.at[g, t], attn_recv.at[g, t]))
        a_high, a_low = halves(attn_buf[g].reshape(rows, HDIM))
        w_high, w_low = halves(head_rows(g))
        for c in range(2):
            cols = slice(c * width, (c + 1) * width)
            m_buf[c] += bf16_dot(a_high, w_high[:, cols], NN) + (
                bf16_dot(a_high, w_low[:, cols], NN) + bf16_dot(a_low, w_high[:, cols], NN)
            )

    loop(pairs, partial_mixed)
    m_copy = remote(
        m_buf.at[1 - side], m_recv, m_send.at[0], m_recv_sem.at[0], me_s, partner
    )
    m_copy.start()

    def g_arrived(z):
        loop(seqs, lambda t: arrived(g_buf.at[z, t], g_recv.at[z, t]))

    loop(pairs, g_arrived)
    incoming = jnp.sum(g_buf[...], axis=0).reshape(rows, HDIM)
    delta = jnp.sum(incoming * attn_own[...].reshape(rows, HDIM), axis=-1, keepdims=True)
    dprobs = exact_dot(incoming, v_buf[...].reshape(rows, HDIM), NT)
    probs = p_buf[...]
    dscores = probs * (dprobs - delta)
    dq = split_dot(dscores, k_buf[...], NN) * scale
    dk = split_dot(dscores, q_buf[...], TN) * scale
    dv = split_dot(probs, incoming, TN).reshape(seqs, RUNS, res, HDIM)
    e_out[0, :, :RUNS] = jnp.where(lane, dq, turn(dk)).reshape(seqs, RUNS, res, HDIM)
    e_out[1, :, :RUNS] = jnp.where(lane, turn(dq), dk).reshape(seqs, RUNS, res, HDIM)
    dv_first = dv[:, 0].reshape(rows // 2, HDIM)
    dv_second = dv[:, 1].reshape(rows // 2, HDIM)
    e_out[0, :, RUNS] = jnp.where(lane_half, dv_first, turn(dv_second)).reshape(seqs, res, HDIM)
    e_out[1, :, RUNS] = jnp.where(lane_half, turn(dv_first), dv_second).reshape(seqs, res, HDIM)

    def e_copies(act, t):
        for c in range(2):
            act(
                e_out.at[c, t], e_buf.at[side, to_slot(t)], e_send.at[c, t],
                e_recv.at[side, to_slot(t)], to_seq(t), 2 * pair + c,
            )

    loop(seqs, functools.partial(e_copies, send))

    m_copy.wait_recv()
    mixed_ref[...] = m_buf[side] + m_recv[...]

    for c in range(2):
        for t in range(seqs):
            arrived(e_buf.at[c, t], e_recv.at[c, t])
    grads_ref[...] = e_buf[0] + e_buf[1]

    loop(seqs, functools.partial(pack_copies, sent))
    loop(pairs, functools.partial(w_copies, sent))
    gout_copy.wait_send()
    first = 0
    for distance, held_here, _ in stages:
        def left(j, distance=distance, held_here=held_here, first=first):
            for n, offset in enumerate(held_here):
                share_copy(sent, j, first, n, offset, distance)

        loop(heads, left)
        first += len(held_here)
    loop(pairs, functools.partial(attn_copies, sent))
    loop(pairs, functools.partial(g_copies, sent))
    m_copy.wait_send()
    loop(seqs, functools.partial(e_copies, sent))


def local(queries, keys, values, local_span, wo_local, wo_strided, grad_out):
    seqs, heads = lax.axis_size("seq"), lax.axis_size("head")
    rows, width = grad_out.shape
    res = STRIDE // seqs
    pairs = heads // 2
    share = min(seqs, HALF // 8)
    piece = RUNS * res
    query_key = jnp.concatenate([queries, keys], axis=1).reshape(RUNS, seqs, res, HDIM)
    value_pair = jnp.concatenate([values[: rows // 2], values[rows // 2 :]], axis=1)
    packed = jnp.concatenate([query_key, value_pair.reshape(1, seqs, res, HDIM)], axis=0)
    packed = packed.transpose(1, 0, 2, 3)
    cotangent = grad_out.reshape(RUNS, seqs, res, width).transpose(1, 0, 2, 3)
    cotangent = cotangent.reshape(rows, width)
    vmem = pl.BlockSpec(memory_space=pltpu.VMEM)
    hbm = pl.BlockSpec(memory_space=pl.ANY)
    dma = pltpu.SemaphoreType.DMA
    f32 = jnp.float32
    mixed, grads = pl.pallas_call(
        functools.partial(kernel, seqs, heads, share),
        out_shape=(
            jax.ShapeDtypeStruct((rows, width), f32),
            jax.ShapeDtypeStruct((seqs, RUNS + 1, res, HDIM), f32),
        ),
        in_specs=[pl.BlockSpec(memory_space=pltpu.SMEM), vmem, vmem, hbm, hbm],
        out_specs=(vmem, vmem),
        scratch_shapes=[
            pltpu.VMEM((heads, share, HALF // share, 2 * width), f32),
            pltpu.VMEM((2, seqs, RUNS + 1, res, HDIM), f32),
            pltpu.VMEM((2, rows, width), jnp.bfloat16),
            pltpu.VMEM((rows, HDIM), f32),
            pltpu.VMEM((rows, HDIM), f32),
            pltpu.VMEM((seqs, RUNS, res, HDIM), f32),
            pltpu.VMEM((rows, rows), f32),
            pltpu.VMEM((seqs, piece, HDIM), f32),
            pltpu.VMEM((pairs, seqs, piece, HDIM), f32),
            pltpu.VMEM((pairs, seqs, piece, HDIM), f32),
            pltpu.VMEM((pairs, seqs, piece, HDIM), f32),
            pltpu.VMEM((2, rows, width), f32),
            pltpu.VMEM((rows, width), f32),
            pltpu.VMEM((2, seqs, RUNS + 1, res, HDIM), f32),
            pltpu.VMEM((2, seqs, RUNS + 1, res, HDIM), f32),
            dma((pairs, 2)),
            dma((heads, share)),
            dma((heads, share)),
            dma((2, seqs)),
            dma((2, seqs)),
            dma((1,)),
            dma((1,)),
            dma((pairs, seqs)),
            dma((pairs, seqs)),
            dma((pairs, seqs)),
            dma((pairs, seqs)),
            dma((1,)),
            dma((1,)),
            dma((2, seqs)),
            dma((2, seqs)),
        ],
        compiler_params=pltpu.CompilerParams(
            collective_id=0, has_side_effects=True, vmem_limit_bytes=48 * 1024 * 1024
        ),
        cost_estimate=pl.CostEstimate(
            flops=2 * rows * 2 * width * HDIM * pairs * 5,
            bytes_accessed=16 * rows * width,
            transcendentals=rows * rows,
        ),
    )(local_span, packed, cotangent, wo_local, wo_strided)
    mixed = mixed.reshape(seqs, RUNS, res, width).transpose(1, 0, 2, 3).reshape(rows, width)
    grads = grads.transpose(1, 0, 2, 3).reshape(RUNS + 1, rows // RUNS, HDIM)
    grad_queries = grads[:RUNS, :, :HALF].reshape(rows, HALF)
    grad_keys = grads[:RUNS, :, HALF:].reshape(rows, HALF)
    grad_values = jnp.concatenate([grads[RUNS, :, :HALF], grads[RUNS, :, HALF:]], axis=0)
    return (mixed, grad_queries, grad_keys, grad_values)


def solution(mesh):
    return jax.shard_map(
        local,
        mesh=mesh,
        in_specs=(
            P("seq", "head"),
            P("seq", "head"),
            P("seq", "head"),
            P(),
            P("head", None),
            P("head", None),
            P("seq", "head"),
        ),
        out_specs=(P("seq", "head"), P("seq", "head"), P("seq", "head"), P("seq", "head")),
        check_vma=False,
    )
```

```python
import functools

import jax
import jax.numpy as jnp
from jax import lax
from jax.experimental import pallas as pl
from jax.experimental.pallas import tpu as pltpu
from jax.sharding import PartitionSpec as P

HDIM = 128
STRIDE = 128
HALF = HDIM // 2
RUNS = 2
HIGHEST = lax.Precision.HIGHEST
NN = (((1,), (0,)), ((), ()))
NT = (((1,), (1,)), ((), ()))
TN = (((0,), (0,)), ((), ()))


def exact_dot(a, b, dims):
    return lax.dot_general(a, b, dims, precision=HIGHEST, preferred_element_type=jnp.float32)


def bf16_dot(a, b, dims):
    return lax.dot_general(a, b, dims, preferred_element_type=jnp.float32)


def halves(x):
    high = x.astype(jnp.bfloat16)
    return high, (x - high.astype(jnp.float32)).astype(jnp.bfloat16)


def split_dot(a, b, dims):
    (a_high, a_low), (b_high, b_low) = halves(a), halves(b)
    return bf16_dot(a_high, b_high, dims) + (
        bf16_dot(a_high, b_low, dims) + bf16_dot(a_low, b_high, dims)
    )


def kernel(
    seqs, heads, share,
    span_ref, query_ref, key_ref, value_ref, gout_ref, wo_local_ref, wo_strided_ref,
    mixed_ref, grad_query_ref, grad_key_ref, grad_value_ref,
    w_buf, pack_ref, pack_buf, gout_buf, q_buf, k_buf, v_buf, p_buf, attn_own, attn_buf,
    gpart, g_buf, m_buf, m_recv, e_out, e_buf,
    w_send, w_recv, share_send, pack_send, pack_recv, gout_send, gout_recv,
    attn_send, attn_recv, g_send, g_recv, m_send, m_recv_sem, e_send, e_recv,
):
    pairs = heads // 2
    res = STRIDE // seqs
    rows = seqs * RUNS * res
    w_rows = HALF // share
    width = gout_ref.shape[1]
    me_s = lax.axis_index("seq")
    me_h = lax.axis_index("head")
    pair = lax.div(me_h, 2)
    side = lax.rem(me_h, 2)
    partner = me_h + 1 - 2 * side
    quarter = lax.rem(me_s, share)

    def to_seq(t):
        return (1 - side) * me_s + side * t

    def to_slot(t):
        return (1 - side) * t + side * me_s

    def flip(value, distance):
        return value + distance - 2 * distance * lax.rem(lax.div(value, distance), 2)

    def exclusive(one, two):
        total, bit = one + two, 1
        while bit < pairs:
            total = total - 2 * bit * lax.rem(lax.div(one, bit), 2) * lax.rem(lax.div(two, bit), 2)
            bit *= 2
        return total

    def is_me(s, h):
        return jnp.logical_and(s == me_s, h == me_h)

    def remote(src, dst, send_sem, recv_sem, s, h):
        return pltpu.make_async_remote_copy(
            src_ref=src, dst_ref=dst, send_sem=send_sem, recv_sem=recv_sem,
            device_id=(s, h), device_id_type=pl.DeviceIdType.MESH,
        )

    def send(src, dst, send_sem, recv_sem, s, h):
        same = is_me(s, h)

        @pl.when(same)
        def _():
            pltpu.make_async_copy(src, dst, recv_sem).start()

        @pl.when(jnp.logical_not(same))
        def _():
            remote(src, dst, send_sem, recv_sem, s, h).start()

    def sent(src, dst, send_sem, recv_sem, s, h):
        @pl.when(jnp.logical_not(is_me(s, h)))
        def _():
            remote(src, dst, send_sem, recv_sem, s, h).wait_send()

    def arrived(dst, recv_sem):
        pltpu.make_async_copy(dst, dst, recv_sem).wait()

    def loop(count, body):
        def step(i, carry):
            body(i)
            return carry
        lax.fori_loop(0, count, step, 0)

    barrier = pltpu.get_barrier_semaphore()

    def greet(i):
        s, h = lax.div(i, heads), lax.rem(i, heads)
        near = jnp.logical_or(s == me_s, lax.div(h, 2) == pair)
        odd = jnp.logical_and(lax.rem(h, 2) == 1, side == 1)
        wanted = jnp.logical_or(near, odd)

        @pl.when(jnp.logical_and(wanted, jnp.logical_not(is_me(s, h))))
        def _():
            pl.semaphore_signal(
                barrier, inc=1, device_id=(s, h), device_id_type=pl.DeviceIdType.MESH
            )

    loop(seqs * heads, greet)

    query_key = jnp.concatenate([query_ref[...], key_ref[...]], axis=0).T
    for a in range(RUNS):
        pack_ref[:, a] = query_key[a * STRIDE : (a + 1) * STRIDE].reshape(seqs, res, HDIM)
    value_pair = jnp.concatenate([value_ref[:, :STRIDE], value_ref[:, STRIDE:]], axis=0).T
    pack_ref[:, RUNS] = value_pair.reshape(seqs, res, HDIM)

    pl.semaphore_wait(
        barrier, heads - 1 + 2 * (seqs - 1) + side * (seqs - 1) * (pairs - 1)
    )

    def pack_copies(act, t):
        for other in range(2):
            s = (1 - other) * me_s + other * t
            slot = (1 - other) * t + other * me_s
            act(
                pack_ref.at[t], pack_buf.at[side, slot], pack_send.at[other, t],
                pack_recv.at[side, slot], s, 2 * pair + other,
            )

    loop(seqs, functools.partial(pack_copies, send))

    def w_copies(act, step):
        z = exclusive(step, pair)
        own_rows = pl.ds(pl.multiple_of(quarter * w_rows, 8), w_rows)
        cols = pl.ds(pl.multiple_of(z * 2 * width, 128), 2 * width)
        for other, source in ((0, wo_local_ref), (1, wo_strided_ref)):
            act(
                source.at[own_rows, cols], w_buf.at[me_h, quarter], w_send.at[z, other],
                w_recv.at[me_h, quarter], me_s, 2 * z + other,
            )

    loop(pairs, functools.partial(w_copies, send))

    gout_copy = remote(
        gout_ref, gout_buf.at[side], gout_send.at[0], gout_recv.at[0], me_s, partner
    )
    gout_copy.start()
    gout_buf[side] = gout_ref[...]

    def share_copy(act, j, stage, offset_at, offset, distance):
        q = quarter
        for bit in (1, 2, 4, 8, 16, 32):
            if offset & bit:
                q = flip(q, bit)
        act(
            w_buf.at[j, q], w_buf.at[j, q], share_send.at[j, stage + offset_at],
            w_recv.at[j, q], flip(me_s, distance), me_h,
        )

    def w_arrived(j, offset):
        q = quarter
        for bit in (1, 2, 4, 8, 16, 32):
            if offset & bit:
                q = flip(q, bit)
        arrived(w_buf.at[j, q], w_recv.at[j, q])

    stages, held, fresh, distance = [], [0], [0], share // 2
    while distance:
        stages.append((distance, tuple(held), tuple(fresh)))
        fresh = [offset ^ distance for offset in held]
        held = held + fresh
        distance //= 2

    def run_stage(at, z):
        distance, held_here, fresh_here = stages[at]
        first = sum(len(s[1]) for s in stages[:at])
        for c in range(2):
            j = 2 * z + c
            for n, offset in enumerate(held_here):
                if offset in fresh_here:
                    w_arrived(j, offset)
                share_copy(send, j, first, n, offset, distance)

    def head_rows(g):
        return w_buf[pl.ds(2 * g, 2)].reshape(HDIM, 2 * width)

    def g_copies(act, g):
        def one(t):
            act(
                gpart.at[g, t], g_buf.at[pair, to_slot(t)], g_send.at[g, t],
                g_recv.at[pair, to_slot(t)], to_seq(t), 2 * g + side,
            )

        loop(seqs, one)

    def partial_grad(g):
        for offset in fresh:
            for c in range(2):
                w_arrived(2 * g + c, offset)
        w_high, w_low = halves(head_rows(g))
        total = jnp.zeros((rows, HDIM), jnp.float32)
        for c in range(2):
            cols = slice(c * width, (c + 1) * width)
            out = gout_buf[c]
            total = total + (
                bf16_dot(out, w_high[:, cols], NT) + bf16_dot(out, w_low[:, cols], NT)
            )
        for a in range(RUNS):
            gpart[g, :, a] = total[a * STRIDE : (a + 1) * STRIDE].reshape(seqs, res, HDIM)
        g_copies(send, g)

    def w_step(step):
        for at in range(len(stages) + 1):
            turn_of = step - at

            @pl.when(jnp.logical_and(turn_of >= 0, turn_of < pairs))
            def _(at=at, turn_of=turn_of):
                z = exclusive(turn_of, pair)
                if at < len(stages):
                    run_stage(at, z)
                else:
                    partial_grad(z)

    ahead = min(2, len(stages))

    loop(ahead, w_step)

    for c in range(2):
        for t in range(seqs):
            arrived(pack_buf.at[c, t], pack_recv.at[c, t])

    lane = lax.broadcasted_iota(jnp.int32, (rows, HDIM), 1) < HALF
    lane_half = lax.broadcasted_iota(jnp.int32, (rows // 2, HDIM), 1) < HALF

    def turn(x):
        return pltpu.roll(x, HALF, 1)

    qk_first = pack_buf[0, :, :RUNS].reshape(rows, HDIM)
    qk_second = pack_buf[1, :, :RUNS].reshape(rows, HDIM)
    q_buf[...] = jnp.where(lane, qk_first, turn(qk_second))
    k_buf[...] = jnp.where(lane, turn(qk_first), qk_second)
    v_first = pack_buf[0, :, RUNS].reshape(rows // 2, HDIM)
    v_second = pack_buf[1, :, RUNS].reshape(rows // 2, HDIM)
    v_buf[:, 0] = jnp.where(lane_half, v_first, turn(v_second)).reshape(seqs, res, HDIM)
    v_buf[:, 1] = jnp.where(lane_half, turn(v_first), v_second).reshape(seqs, res, HDIM)

    res_bits = res.bit_length() - 1

    def place(dim):
        index = lax.broadcasted_iota(jnp.int32, (rows, rows), dim)
        run = (index >> res_bits) & 1
        part = index >> (res_bits + 1)
        residue = index & (res - 1)
        return run, part, residue

    run_i, part_i, residue_i = place(0)
    run_j, part_j, residue_j = place(1)
    at_i = run_i * STRIDE + part_i * res + residue_i
    at_j = run_j * STRIDE + part_j * res + residue_j
    local_ok = jnp.where((at_j <= at_i) & (run_i - run_j < span_ref[pair]), 1, 0)
    order_ok = RUNS * part_j + run_j <= RUNS * part_i + run_i
    strided_ok = jnp.where((residue_i == residue_j) & order_ok, 1, 0)
    allowed = local_ok * (1 - side) + strided_ok * side > 0

    scale = HDIM ** (-0.5)
    scores = exact_dot(q_buf[...], k_buf[...], NT) * scale
    row_max = jnp.max(jnp.where(allowed, scores, -jnp.inf), axis=-1, keepdims=True)
    weights = jnp.where(allowed, jnp.exp(scores - row_max), 0.0)
    probs = weights / jnp.sum(weights, axis=-1, keepdims=True)
    p_buf[...] = probs
    attended = exact_dot(probs, v_buf[...].reshape(rows, HDIM), NN)
    attn_own[...] = attended.reshape(seqs, RUNS, res, HDIM)

    def attn_copies(act, step):
        z = exclusive(step, pair)

        def one(t):
            act(
                attn_own.at[t], attn_buf.at[pair, to_slot(t)], attn_send.at[z, t],
                attn_recv.at[pair, to_slot(t)], to_seq(t), 2 * z + side,
            )

        loop(seqs, one)

    loop(pairs, functools.partial(attn_copies, send))

    gout_copy.wait_recv()

    def rest(step):
        w_step(step + ahead)

    loop(pairs + len(stages) - ahead, rest)

    m_buf[...] = jnp.zeros_like(m_buf)

    def partial_mixed(step):
        g = exclusive(step, pair)
        loop(seqs, lambda t: arrived(attn_buf.at[g, t], attn_recv.at[g, t]))
        attn = jnp.concatenate(
            [attn_buf[g, :, a].reshape(STRIDE, HDIM) for a in range(RUNS)], axis=0
        )
        a_high, a_low = halves(attn)
        w_high, w_low = halves(head_rows(g))
        for c in range(2):
            cols = slice(c * width, (c + 1) * width)
            m_buf[c] += bf16_dot(a_high, w_high[:, cols], NN) + (
                bf16_dot(a_high, w_low[:, cols], NN) + bf16_dot(a_low, w_high[:, cols], NN)
            )

    loop(pairs, partial_mixed)
    m_copy = remote(
        m_buf.at[1 - side], m_recv, m_send.at[0], m_recv_sem.at[0], me_s, partner
    )
    m_copy.start()

    def g_arrived(z):
        loop(seqs, lambda t: arrived(g_buf.at[z, t], g_recv.at[z, t]))

    loop(pairs, g_arrived)
    incoming = jnp.sum(g_buf[...], axis=0).reshape(rows, HDIM)
    delta = jnp.sum(incoming * attn_own[...].reshape(rows, HDIM), axis=-1, keepdims=True)
    dprobs = exact_dot(incoming, v_buf[...].reshape(rows, HDIM), NT)
    probs = p_buf[...]
    dscores = probs * (dprobs - delta)
    dq = split_dot(dscores, k_buf[...], NN) * scale
    dk = split_dot(dscores, q_buf[...], TN) * scale
    dv = split_dot(probs, incoming, TN).reshape(seqs, RUNS, res, HDIM)
    e_out[0, :, :RUNS] = jnp.where(lane, dq, turn(dk)).reshape(seqs, RUNS, res, HDIM)
    e_out[1, :, :RUNS] = jnp.where(lane, turn(dq), dk).reshape(seqs, RUNS, res, HDIM)
    dv_first = dv[:, 0].reshape(rows // 2, HDIM)
    dv_second = dv[:, 1].reshape(rows // 2, HDIM)
    e_out[0, :, RUNS] = jnp.where(lane_half, dv_first, turn(dv_second)).reshape(seqs, res, HDIM)
    e_out[1, :, RUNS] = jnp.where(lane_half, turn(dv_first), dv_second).reshape(seqs, res, HDIM)

    def e_copies(act, t):
        for c in range(2):
            act(
                e_out.at[c, t], e_buf.at[side, to_slot(t)], e_send.at[c, t],
                e_recv.at[side, to_slot(t)], to_seq(t), 2 * pair + c,
            )

    loop(seqs, functools.partial(e_copies, send))

    m_copy.wait_recv()
    mixed_ref[...] = m_buf[side] + m_recv[...]

    for c in range(2):
        for t in range(seqs):
            arrived(e_buf.at[c, t], e_recv.at[c, t])
    grads = e_buf[0] + e_buf[1]
    query_key = jnp.concatenate([grads[:, a].reshape(STRIDE, HDIM) for a in range(RUNS)], axis=0).T
    grad_query_ref[...] = query_key[:HALF]
    grad_key_ref[...] = query_key[HALF:]
    value_pair = grads[:, RUNS].reshape(STRIDE, HDIM).T
    grad_value_ref[:, :STRIDE] = value_pair[:HALF]
    grad_value_ref[:, STRIDE:] = value_pair[HALF:]

    loop(seqs, functools.partial(pack_copies, sent))
    loop(pairs, functools.partial(w_copies, sent))
    gout_copy.wait_send()
    first = 0
    for distance, held_here, _ in stages:
        def left(j, distance=distance, held_here=held_here, first=first):
            for n, offset in enumerate(held_here):
                share_copy(sent, j, first, n, offset, distance)

        loop(heads, left)
        first += len(held_here)
    loop(pairs, functools.partial(attn_copies, sent))
    loop(pairs, functools.partial(g_copies, sent))
    m_copy.wait_send()
    loop(seqs, functools.partial(e_copies, sent))


def local(queries, keys, values, local_span, wo_local, wo_strided, grad_out):
    seqs, heads = lax.axis_size("seq"), lax.axis_size("head")
    rows, width = grad_out.shape
    res = STRIDE // seqs
    pairs = heads // 2
    share = min(seqs, HALF // 8)
    vmem = pl.BlockSpec(memory_space=pltpu.VMEM)
    hbm = pl.BlockSpec(memory_space=pl.ANY)
    dma = pltpu.SemaphoreType.DMA
    f32 = jnp.float32
    mixed, grad_queries, grad_keys, grad_values = pl.pallas_call(
        functools.partial(kernel, seqs, heads, share),
        out_shape=(
            jax.ShapeDtypeStruct((rows, width), f32),
            jax.ShapeDtypeStruct((HALF, rows), f32),
            jax.ShapeDtypeStruct((HALF, rows), f32),
            jax.ShapeDtypeStruct((HALF, rows), f32),
        ),
        in_specs=[pl.BlockSpec(memory_space=pltpu.SMEM), vmem, vmem, vmem, vmem, hbm, hbm],
        out_specs=(vmem, vmem, vmem, vmem),
        scratch_shapes=[
            pltpu.VMEM((heads, share, HALF // share, 2 * width), f32),
            pltpu.VMEM((seqs, RUNS + 1, res, HDIM), f32),
            pltpu.VMEM((2, seqs, RUNS + 1, res, HDIM), f32),
            pltpu.VMEM((2, rows, width), jnp.bfloat16),
            pltpu.VMEM((rows, HDIM), f32),
            pltpu.VMEM((rows, HDIM), f32),
            pltpu.VMEM((seqs, RUNS, res, HDIM), f32),
            pltpu.VMEM((rows, rows), f32),
            pltpu.VMEM((seqs, RUNS, res, HDIM), f32),
            pltpu.VMEM((pairs, seqs, RUNS, res, HDIM), f32),
            pltpu.VMEM((pairs, seqs, RUNS, res, HDIM), f32),
            pltpu.VMEM((pairs, seqs, RUNS, res, HDIM), f32),
            pltpu.VMEM((2, rows, width), f32),
            pltpu.VMEM((rows, width), f32),
            pltpu.VMEM((2, seqs, RUNS + 1, res, HDIM), f32),
            pltpu.VMEM((2, seqs, RUNS + 1, res, HDIM), f32),
            dma((pairs, 2)),
            dma((heads, share)),
            dma((heads, share)),
            dma((2, seqs)),
            dma((2, seqs)),
            dma((1,)),
            dma((1,)),
            dma((pairs, seqs)),
            dma((pairs, seqs)),
            dma((pairs, seqs)),
            dma((pairs, seqs)),
            dma((1,)),
            dma((1,)),
            dma((2, seqs)),
            dma((2, seqs)),
        ],
        compiler_params=pltpu.CompilerParams(
            collective_id=0, has_side_effects=True, vmem_limit_bytes=60 * 1024 * 1024
        ),
        cost_estimate=pl.CostEstimate(
            flops=2 * rows * 2 * width * HDIM * pairs * 5,
            bytes_accessed=16 * rows * width,
            transcendentals=rows * rows,
        ),
    )(local_span, queries.T, keys.T, values.T, grad_out, wo_local, wo_strided)
    return (mixed, grad_queries.T, grad_keys.T, grad_values.T)


def solution(mesh):
    return jax.shard_map(
        local,
        mesh=mesh,
        in_specs=(
            P("seq", "head"),
            P("seq", "head"),
            P("seq", "head"),
            P(),
            P("head", None),
            P("head", None),
            P("seq", "head"),
        ),
        out_specs=(P("seq", "head"), P("seq", "head"), P("seq", "head"), P("seq", "head")),
        check_vma=False,
    )
```

```python
import functools

import jax
import jax.numpy as jnp
from jax import lax
from jax.experimental import pallas as pl
from jax.experimental.pallas import tpu as pltpu
from jax.sharding import PartitionSpec as P

HDIM = 128
STRIDE = 128
HALF = HDIM // 2
RUNS = 2
HIGHEST = lax.Precision.HIGHEST
NN = (((1,), (0,)), ((), ()))
NT = (((1,), (1,)), ((), ()))
TN = (((0,), (0,)), ((), ()))


def exact_dot(a, b, dims):
    return lax.dot_general(a, b, dims, precision=HIGHEST, preferred_element_type=jnp.float32)


def bf16_dot(a, b, dims):
    return lax.dot_general(a, b, dims, preferred_element_type=jnp.float32)


def halves(x):
    high = x.astype(jnp.bfloat16)
    return high, (x - high.astype(jnp.float32)).astype(jnp.bfloat16)


def split_dot(a, b, dims):
    (a_high, a_low), (b_high, b_low) = halves(a), halves(b)
    return bf16_dot(a_high, b_high, dims) + (
        bf16_dot(a_high, b_low, dims) + bf16_dot(a_low, b_high, dims)
    )


def kernel(
    seqs, heads, share,
    span_ref, query_ref, key_ref, value_ref, gout_ref, wo_local_ref, wo_strided_ref,
    mixed_ref, grad_query_ref, grad_key_ref, grad_value_ref,
    w_buf, pack_ref, pack_buf, gout_buf, q_buf, k_buf, v_buf, p_buf, attn_own, attn_buf,
    gpart, g_buf, m_buf, m_recv, e_out, e_buf,
    w_send, w_recv, share_send, pack_send, pack_recv, gout_send, gout_recv,
    attn_send, attn_recv, g_send, g_recv, m_send, m_recv_sem, e_send, e_recv,
):
    pairs = heads // 2
    res = STRIDE // seqs
    rows = seqs * RUNS * res
    w_rows = HALF // share
    width = gout_ref.shape[1]
    me_s = lax.axis_index("seq")
    me_h = lax.axis_index("head")
    pair = lax.div(me_h, 2)
    side = lax.rem(me_h, 2)
    partner = me_h + 1 - 2 * side
    quarter = lax.rem(me_s, share)

    def to_seq(t):
        return (1 - side) * me_s + side * t

    def to_slot(t):
        return (1 - side) * t + side * me_s

    def flip(value, distance):
        return value + distance - 2 * distance * lax.rem(lax.div(value, distance), 2)

    def exclusive(one, two):
        total, bit = one + two, 1
        while bit < pairs:
            total = total - 2 * bit * lax.rem(lax.div(one, bit), 2) * lax.rem(lax.div(two, bit), 2)
            bit *= 2
        return total

    def is_me(s, h):
        return jnp.logical_and(s == me_s, h == me_h)

    def remote(src, dst, send_sem, recv_sem, s, h):
        return pltpu.make_async_remote_copy(
            src_ref=src, dst_ref=dst, send_sem=send_sem, recv_sem=recv_sem,
            device_id=(s, h), device_id_type=pl.DeviceIdType.MESH,
        )

    def send(src, dst, send_sem, recv_sem, s, h):
        same = is_me(s, h)

        @pl.when(same)
        def _():
            pltpu.make_async_copy(src, dst, recv_sem).start()

        @pl.when(jnp.logical_not(same))
        def _():
            remote(src, dst, send_sem, recv_sem, s, h).start()

    def arrived(like, sem):
        pltpu.make_async_copy(like, like, sem).wait()

    def loop(count, body):
        def step(i, carry):
            body(i)
            return carry
        lax.fori_loop(0, count, step, 0)

    barrier = pltpu.get_barrier_semaphore()

    def greet(s, h):
        pl.semaphore_signal(
            barrier, inc=1, device_id=(s, h), device_id_type=pl.DeviceIdType.MESH
        )

    loop(heads - 1, lambda i: greet(me_s, lax.rem(me_h + 1 + i, heads)))

    def greet_seq(i):
        s = lax.rem(me_s + 1 + i, seqs)
        greet(s, me_h)
        greet(s, partner)

        @pl.when(side == 1)
        def _():
            loop(pairs - 1, lambda n: greet(s, lax.rem(me_h + 2 + 2 * n, heads)))

    loop(seqs - 1, greet_seq)

    query_key = jnp.concatenate([query_ref[...], key_ref[...]], axis=0).T
    for a in range(RUNS):
        pack_ref[:, a] = query_key[a * STRIDE : (a + 1) * STRIDE].reshape(seqs, res, HDIM)
    value_pair = jnp.concatenate([value_ref[:, :STRIDE], value_ref[:, STRIDE:]], axis=0).T
    pack_ref[:, RUNS] = value_pair.reshape(seqs, res, HDIM)

    pl.semaphore_wait(
        barrier, heads - 1 + 2 * (seqs - 1) + side * (seqs - 1) * (pairs - 1)
    )

    def pack_copies(t):
        for other in range(2):
            s = (1 - other) * me_s + other * t
            slot = (1 - other) * t + other * me_s
            send(
                pack_ref.at[t], pack_buf.at[side, slot], pack_send.at[other],
                pack_recv.at[0], s, 2 * pair + other,
            )

    loop(seqs, pack_copies)

    def w_copies(step):
        z = exclusive(step, pair)
        own_rows = pl.ds(pl.multiple_of(quarter * w_rows, 8), w_rows)
        cols = pl.ds(pl.multiple_of(z * 2 * width, 128), 2 * width)
        for other, source in ((0, wo_local_ref), (1, wo_strided_ref)):
            send(
                source.at[own_rows, cols], w_buf.at[me_h, quarter], w_send.at[0],
                w_recv.at[pair, quarter], me_s, 2 * z + other,
            )

    loop(pairs, w_copies)

    gout_copy = remote(
        gout_ref, gout_buf.at[side], gout_send.at[0], gout_recv.at[0], me_s, partner
    )
    gout_copy.start()
    gout_buf[side] = gout_ref[...]

    def row_part(offset):
        q = quarter
        for bit in (1, 2, 4, 8, 16, 32):
            if offset & bit:
                q = flip(q, bit)
        return q

    def w_part(z, offset):
        return w_buf.at[pl.ds(2 * z, 2), row_part(offset)]

    def w_arrived(z, offset):
        arrived(w_part(z, offset), w_recv.at[z, row_part(offset)])

    stages, held, fresh, distance = [], [0], [0], share // 2
    while distance:
        stages.append((distance, tuple(held), tuple(fresh)))
        fresh = [offset ^ distance for offset in held]
        held = held + fresh
        distance //= 2

    def run_stage(at, z):
        distance, held_here, fresh_here = stages[at]
        for offset in held_here:
            if offset in fresh_here:
                w_arrived(z, offset)
            remote(
                w_part(z, offset), w_part(z, offset), share_send.at[at],
                w_recv.at[z, row_part(offset)], flip(me_s, distance), me_h,
            ).start()

    def head_rows(g):
        return w_buf[pl.ds(2 * g, 2)].reshape(HDIM, 2 * width)

    def own_or_other(sems, z):
        return sems.at[jnp.where(z == pair, 1, 0)]

    def g_copies(g):
        def one(t):
            send(
                gpart.at[g, t], g_buf.at[pair, to_slot(t)], own_or_other(g_send, g),
                g_recv.at[0], to_seq(t), 2 * g + side,
            )

        loop(seqs, one)

    def partial_grad(g):
        for offset in fresh:
            w_arrived(g, offset)
        w_high, w_low = halves(head_rows(g))
        total = jnp.zeros((rows, HDIM), jnp.float32)
        for c in range(2):
            cols = slice(c * width, (c + 1) * width)
            out = gout_buf[c]
            total = total + (
                bf16_dot(out, w_high[:, cols], NT) + bf16_dot(out, w_low[:, cols], NT)
            )
        for a in range(RUNS):
            gpart[g, :, a] = total[a * STRIDE : (a + 1) * STRIDE].reshape(seqs, res, HDIM)
        g_copies(g)

    def w_step(step):
        for at in range(len(stages) + 1):
            turn_of = step - at - at // len(stages)

            @pl.when(jnp.logical_and(turn_of >= 0, turn_of < pairs))
            def _(at=at, turn_of=turn_of):
                z = exclusive(turn_of, pair)
                if at < len(stages):
                    run_stage(at, z)
                else:
                    partial_grad(z)

    ahead = 2

    loop(ahead, w_step)

    arrived(pack_buf, pack_recv.at[0])

    lane = lax.broadcasted_iota(jnp.int32, (rows, HDIM), 1) < HALF
    lane_half = lax.broadcasted_iota(jnp.int32, (rows // 2, HDIM), 1) < HALF

    def turn(x):
        return pltpu.roll(x, HALF, 1)

    qk_first = pack_buf[0, :, :RUNS].reshape(rows, HDIM)
    qk_second = pack_buf[1, :, :RUNS].reshape(rows, HDIM)
    q_buf[...] = jnp.where(lane, qk_first, turn(qk_second))
    k_buf[...] = jnp.where(lane, turn(qk_first), qk_second)
    v_first = pack_buf[0, :, RUNS].reshape(rows // 2, HDIM)
    v_second = pack_buf[1, :, RUNS].reshape(rows // 2, HDIM)
    v_buf[:, 0] = jnp.where(lane_half, v_first, turn(v_second)).reshape(seqs, res, HDIM)
    v_buf[:, 1] = jnp.where(lane_half, turn(v_first), v_second).reshape(seqs, res, HDIM)

    res_bits = res.bit_length() - 1

    def place(dim):
        index = lax.broadcasted_iota(jnp.int32, (rows, rows), dim)
        run = (index >> res_bits) & 1
        part = index >> (res_bits + 1)
        residue = index & (res - 1)
        return run, part, residue

    run_i, part_i, residue_i = place(0)
    run_j, part_j, residue_j = place(1)
    at_i = run_i * STRIDE + part_i * res + residue_i
    at_j = run_j * STRIDE + part_j * res + residue_j
    local_ok = jnp.where((at_j <= at_i) & (run_i - run_j < span_ref[pair]), 1, 0)
    order_ok = RUNS * part_j + run_j <= RUNS * part_i + run_i
    strided_ok = jnp.where((residue_i == residue_j) & order_ok, 1, 0)
    allowed = local_ok * (1 - side) + strided_ok * side > 0

    scale = HDIM ** (-0.5)
    scores = exact_dot(q_buf[...], k_buf[...], NT) * scale
    row_max = jnp.max(jnp.where(allowed, scores, -jnp.inf), axis=-1, keepdims=True)
    weights = jnp.where(allowed, jnp.exp(scores - row_max), 0.0)
    probs = weights / jnp.sum(weights, axis=-1, keepdims=True)
    p_buf[...] = probs
    w_step(ahead)
    attended = exact_dot(probs, v_buf[...].reshape(rows, HDIM), NN)
    attn_own[...] = attended.reshape(seqs, RUNS, res, HDIM)

    def attn_copies(step):
        z = exclusive(step, pair)

        def one(t):
            send(
                attn_own.at[t], attn_buf.at[pair, to_slot(t)], own_or_other(attn_send, z),
                attn_recv.at[pair], to_seq(t), 2 * z + side,
            )

        loop(seqs, one)

    loop(pairs, attn_copies)

    gout_copy.wait_recv()

    def rest(step):
        w_step(step + ahead + 1)

    loop(pairs + len(stages) - ahead, rest)

    m_buf[...] = jnp.zeros_like(m_buf)

    def partial_mixed(step):
        g = exclusive(step, pair)
        arrived(attn_buf.at[g], attn_recv.at[g])
        attn = jnp.concatenate(
            [attn_buf[g, :, a].reshape(STRIDE, HDIM) for a in range(RUNS)], axis=0
        )
        a_high, a_low = halves(attn)
        w_high, w_low = halves(head_rows(g))
        for c in range(2):
            cols = slice(c * width, (c + 1) * width)
            m_buf[c] += bf16_dot(a_high, w_high[:, cols], NN) + (
                bf16_dot(a_high, w_low[:, cols], NN) + bf16_dot(a_low, w_high[:, cols], NN)
            )

    loop(pairs, partial_mixed)
    m_copy = remote(
        m_buf.at[1 - side], m_recv, m_send.at[0], m_recv_sem.at[0], me_s, partner
    )
    m_copy.start()

    arrived(g_buf, g_recv.at[0])
    incoming = jnp.sum(g_buf[...], axis=0).reshape(rows, HDIM)
    delta = jnp.sum(incoming * attn_own[...].reshape(rows, HDIM), axis=-1, keepdims=True)
    dprobs = exact_dot(incoming, v_buf[...].reshape(rows, HDIM), NT)
    probs = p_buf[...]
    dscores = probs * (dprobs - delta)
    dq = split_dot(dscores, k_buf[...], NN) * scale
    dk = split_dot(dscores, q_buf[...], TN) * scale
    dv = split_dot(probs, incoming, TN).reshape(seqs, RUNS, res, HDIM)
    e_out[0, :, :RUNS] = jnp.where(lane, dq, turn(dk)).reshape(seqs, RUNS, res, HDIM)
    e_out[1, :, :RUNS] = jnp.where(lane, turn(dq), dk).reshape(seqs, RUNS, res, HDIM)
    dv_first = dv[:, 0].reshape(rows // 2, HDIM)
    dv_second = dv[:, 1].reshape(rows // 2, HDIM)
    e_out[0, :, RUNS] = jnp.where(lane_half, dv_first, turn(dv_second)).reshape(seqs, res, HDIM)
    e_out[1, :, RUNS] = jnp.where(lane_half, turn(dv_first), dv_second).reshape(seqs, res, HDIM)

    def e_copies(t):
        for c in range(2):
            send(
                e_out.at[c, t], e_buf.at[side, to_slot(t)], e_send.at[c],
                e_recv.at[0], to_seq(t), 2 * pair + c,
            )

    loop(seqs, e_copies)

    arrived(pack_ref, pack_send.at[1 - side])
    arrived(w_buf.at[pl.ds(0, heads - 1), 0], w_send.at[0])
    gout_copy.wait_send()
    for at, (_, held_here, _) in enumerate(stages):
        arrived(w_buf.at[:, pl.ds(0, len(held_here))], share_send.at[at])
    arrived(attn_buf.at[pl.ds(0, pairs - 1)], attn_send.at[0])
    arrived(gpart.at[pl.ds(0, pairs - 1)], g_send.at[0])

    @pl.when(side == 1)
    def _():
        arrived(pack_ref.at[pl.ds(0, seqs - 1)], pack_send.at[1])
        arrived(attn_own.at[pl.ds(0, seqs - 1)], attn_send.at[1])
        arrived(attn_own.at[pl.ds(0, seqs - 1)], g_send.at[1])

    m_copy.wait_recv()
    mixed_ref[...] = m_buf[side] + m_recv[...]

    arrived(e_buf, e_recv.at[0])
    grads = e_buf[0] + e_buf[1]
    query_key = jnp.concatenate([grads[:, a].reshape(STRIDE, HDIM) for a in range(RUNS)], axis=0).T
    grad_query_ref[...] = query_key[:HALF]
    grad_key_ref[...] = query_key[HALF:]
    value_pair = grads[:, RUNS].reshape(STRIDE, HDIM).T
    grad_value_ref[:, :STRIDE] = value_pair[:HALF]
    grad_value_ref[:, STRIDE:] = value_pair[HALF:]

    m_copy.wait_send()
    arrived(e_out.at[0], e_send.at[1 - side])

    @pl.when(side == 1)
    def _():
        arrived(e_out.at[0, pl.ds(0, seqs - 1)], e_send.at[1])


def write_kernel(*refs):
    count = len(refs) // 2
    sems = refs[-1]
    copies = [pltpu.make_async_copy(refs[i], refs[count + i], sems.at[i]) for i in range(count)]
    for copy in copies:
        copy.start()
    for copy in copies:
        copy.wait()


def local(queries, keys, values, local_span, wo_local, wo_strided, grad_out):
    seqs, heads = lax.axis_size("seq"), lax.axis_size("head")
    rows, width = grad_out.shape
    res = STRIDE // seqs
    pairs = heads // 2
    share = min(seqs, HALF // 8)
    vmem = pl.BlockSpec(memory_space=pltpu.VMEM)
    hbm = pl.BlockSpec(memory_space=pltpu.HBM)
    dma = pltpu.SemaphoreType.DMA
    f32 = jnp.float32
    results = pl.pallas_call(
        functools.partial(kernel, seqs, heads, share),
        out_shape=(
            jax.ShapeDtypeStruct((rows, width), f32),
            jax.ShapeDtypeStruct((HALF, rows), f32),
            jax.ShapeDtypeStruct((HALF, rows), f32),
            jax.ShapeDtypeStruct((HALF, rows), f32),
        ),
        in_specs=[pl.BlockSpec(memory_space=pltpu.SMEM), vmem, vmem, vmem, vmem, hbm, hbm],
        out_specs=(vmem, vmem, vmem, vmem),
        scratch_shapes=[
            pltpu.VMEM((heads, share, HALF // share, 2 * width), f32),
            pltpu.VMEM((seqs, RUNS + 1, res, HDIM), f32),
            pltpu.VMEM((2, seqs, RUNS + 1, res, HDIM), f32),
            pltpu.VMEM((2, rows, width), jnp.bfloat16),
            pltpu.VMEM((rows, HDIM), f32),
            pltpu.VMEM((rows, HDIM), f32),
            pltpu.VMEM((seqs, RUNS, res, HDIM), f32),
            pltpu.VMEM((rows, rows), f32),
            pltpu.VMEM((seqs, RUNS, res, HDIM), f32),
            pltpu.VMEM((pairs, seqs, RUNS, res, HDIM), f32),
            pltpu.VMEM((pairs, seqs, RUNS, res, HDIM), f32),
            pltpu.VMEM((pairs, seqs, RUNS, res, HDIM), f32),
            pltpu.VMEM((2, rows, width), f32),
            pltpu.VMEM((rows, width), f32),
            pltpu.VMEM((2, seqs, RUNS + 1, res, HDIM), f32),
            pltpu.VMEM((2, seqs, RUNS + 1, res, HDIM), f32),
            dma((1,)),
            dma((pairs, share)),
            dma((max(1, share.bit_length() - 1),)),
            dma((2,)),
            dma((1,)),
            dma((1,)),
            dma((1,)),
            dma((2,)),
            dma((pairs,)),
            dma((2,)),
            dma((1,)),
            dma((1,)),
            dma((1,)),
            dma((2,)),
            dma((1,)),
        ],
        compiler_params=pltpu.CompilerParams(
            collective_id=0, has_side_effects=True, vmem_limit_bytes=48 * 1024 * 1024
        ),
        cost_estimate=pl.CostEstimate(
            flops=2 * rows * 2 * width * HDIM * pairs * 5,
            bytes_accessed=16 * rows * width,
            transcendentals=rows * rows,
        ),
    )(local_span, queries.T, keys.T, values.T, grad_out, wo_local, wo_strided)
    anywhere = pl.BlockSpec(memory_space=pl.ANY)
    mixed, grad_queries, grad_keys, grad_values = pl.pallas_call(
        write_kernel,
        out_shape=[jax.ShapeDtypeStruct(x.shape, x.dtype) for x in results],
        in_specs=[anywhere] * len(results),
        out_specs=[hbm] * len(results),
        scratch_shapes=[dma((len(results),))],
    )(*results)
    return (mixed, grad_queries.T, grad_keys.T, grad_values.T)


def solution(mesh):
    return jax.shard_map(
        local,
        mesh=mesh,
        in_specs=(
            P("seq", "head"),
            P("seq", "head"),
            P("seq", "head"),
            P(),
            P("head", None),
            P("head", None),
            P("seq", "head"),
        ),
        out_specs=(P("seq", "head"), P("seq", "head"), P("seq", "head"), P("seq", "head")),
        check_vma=False,
    )
```

```python
import functools

import jax
import jax.numpy as jnp
from jax import lax
from jax.experimental import pallas as pl
from jax.experimental.pallas import tpu as pltpu
from jax.sharding import PartitionSpec as P

HDIM = 128
STRIDE = 128
HALF = HDIM // 2
RUNS = 2
HIGHEST = lax.Precision.HIGHEST
NN = (((1,), (0,)), ((), ()))
NT = (((1,), (1,)), ((), ()))
TN = (((0,), (0,)), ((), ()))


def exact_dot(a, b, dims):
    return lax.dot_general(a, b, dims, precision=HIGHEST, preferred_element_type=jnp.float32)


def bf16_dot(a, b, dims):
    return lax.dot_general(a, b, dims, preferred_element_type=jnp.float32)


def halves(x):
    high = x.astype(jnp.bfloat16)
    return high, (x - high.astype(jnp.float32)).astype(jnp.bfloat16)


def split_dot(a, b, dims):
    (a_high, a_low), (b_high, b_low) = halves(a), halves(b)
    return bf16_dot(a_high, b_high, dims) + (
        bf16_dot(a_high, b_low, dims) + bf16_dot(a_low, b_high, dims)
    )


def kernel(
    seqs, heads, share,
    span_ref, query_ref, key_ref, value_ref, gout_ref, wo_local_ref, wo_strided_ref,
    mixed_ref, grad_query_ref, grad_key_ref, grad_value_ref,
    in_buf, w_buf, pack_ref, pack_buf, gout_buf, q_buf, k_buf, v_buf, p_buf, attn_own, attn_buf,
    gpart, near_buf, g_buf, m_buf, m_recv, e_out, e_buf,
    in_sem, w_send, w_recv, share_send, pack_send, pack_recv, gout_send, gout_recv,
    attn_send, attn_recv, hand_send, near_send, near_recv, g_send, g_recv, m_send, m_recv_sem, e_send, e_recv,
):
    pairs = heads // 2
    res = STRIDE // seqs
    rows = seqs * RUNS * res
    w_rows = HALF // share
    width = gout_ref.shape[1]
    me_s = lax.axis_index("seq")
    me_h = lax.axis_index("head")
    pair = lax.div(me_h, 2)
    side = lax.rem(me_h, 2)
    partner = me_h + 1 - 2 * side
    quarter = lax.rem(me_s, share)

    def to_seq(t):
        return (1 - side) * me_s + side * t

    def to_slot(t):
        return (1 - side) * t + side * me_s

    def flip(value, distance):
        return value + distance - 2 * distance * lax.rem(lax.div(value, distance), 2)

    def exclusive(one, two):
        total, bit = one + two, 1
        while bit < pairs:
            total = total - 2 * bit * lax.rem(lax.div(one, bit), 2) * lax.rem(lax.div(two, bit), 2)
            bit *= 2
        return total

    def is_me(s, h):
        return jnp.logical_and(s == me_s, h == me_h)

    def remote(src, dst, send_sem, recv_sem, s, h):
        return pltpu.make_async_remote_copy(
            src_ref=src, dst_ref=dst, send_sem=send_sem, recv_sem=recv_sem,
            device_id=(s, h), device_id_type=pl.DeviceIdType.MESH,
        )

    def send(src, dst, send_sem, recv_sem, s, h):
        same = is_me(s, h)

        @pl.when(same)
        def _():
            pltpu.make_async_copy(src, dst, recv_sem).start()

        @pl.when(jnp.logical_not(same))
        def _():
            remote(src, dst, send_sem, recv_sem, s, h).start()

    def arrived(like, sem):
        pltpu.make_async_copy(like, like, sem).wait()

    def loop(count, body):
        def step(i, carry):
            body(i)
            return carry
        lax.fori_loop(0, count, step, 0)

    own_inputs = [
        pltpu.make_async_copy(ref, in_buf.at[i], in_sem.at[i])
        for i, ref in enumerate((query_ref, key_ref, value_ref))
    ]
    own_inputs.append(pltpu.make_async_copy(gout_ref, gout_buf.at[side], in_sem.at[3]))
    for copy in own_inputs:
        copy.start()

    barrier = pltpu.get_barrier_semaphore()

    def greet(s, h):
        pl.semaphore_signal(
            barrier, inc=1, device_id=(s, h), device_id_type=pl.DeviceIdType.MESH
        )

    loop(heads - 1, lambda i: greet(me_s, lax.rem(me_h + 1 + i, heads)))

    def greet_seq(i):
        s = lax.rem(me_s + 1 + i, seqs)
        greet(s, me_h)
        greet(s, partner)

        @pl.when(side == 1)
        def _():
            loop(pairs - 1, lambda n: greet(s, lax.rem(me_h + 2 + 2 * n, heads)))

    loop(seqs - 1, greet_seq)

    for copy in own_inputs[:3]:
        copy.wait()
    query_key = in_buf[:2].reshape(HDIM, rows).T
    for a in range(RUNS):
        pack_ref[:, a] = query_key[a * STRIDE : (a + 1) * STRIDE].reshape(seqs, res, HDIM)
    value_pair = jnp.concatenate([in_buf[2, :, :STRIDE], in_buf[2, :, STRIDE:]], axis=0).T
    pack_ref[:, RUNS] = value_pair.reshape(seqs, res, HDIM)

    pl.semaphore_wait(
        barrier, heads - 1 + 2 * (seqs - 1) + side * (seqs - 1) * (pairs - 1)
    )

    def pack_copies(t):
        for other in range(2):
            s = (1 - other) * me_s + other * t
            slot = (1 - other) * t + other * me_s
            send(
                pack_ref.at[t], pack_buf.at[side, slot], pack_send.at[other],
                pack_recv.at[0], s, 2 * pair + other,
            )

    loop(seqs, pack_copies)

    def gray(step):
        return exclusive(step, lax.div(step, 2))

    neighbour = exclusive(1, pair)

    def w_copies(step):
        z = exclusive(gray(step), pair)
        own_rows = pl.ds(pl.multiple_of(quarter * w_rows, 8), w_rows)
        cols = pl.ds(pl.multiple_of(z * 2 * width, 128), 2 * width)
        for other, source in ((0, wo_local_ref), (1, wo_strided_ref)):
            send(
                source.at[own_rows, cols], w_buf.at[me_h, quarter], w_send.at[0],
                w_recv.at[pair, quarter], me_s, 2 * z + other,
            )

    loop(pairs, w_copies)

    gout_copy = remote(
        gout_ref, gout_buf.at[side], gout_send.at[0], gout_recv.at[0], me_s, partner
    )
    gout_copy.start()

    def row_part(offset):
        q = quarter
        for bit in (1, 2, 4, 8, 16, 32):
            if offset & bit:
                q = flip(q, bit)
        return q

    def w_part(z, offset):
        return w_buf.at[pl.ds(2 * z, 2), row_part(offset)]

    def w_arrived(z, offset):
        arrived(w_part(z, offset), w_recv.at[z, row_part(offset)])

    stages, held, fresh, distance = [], [0], [0], share // 2
    while distance:
        stages.append((distance, tuple(held), tuple(fresh)))
        fresh = [offset ^ distance for offset in held]
        held = held + fresh
        distance //= 2

    def run_stage(at, z):
        distance, held_here, fresh_here = stages[at]
        for offset in held_here:
            if offset in fresh_here:
                w_arrived(z, offset)
            remote(
                w_part(z, offset), w_part(z, offset), share_send.at[at],
                w_recv.at[z, row_part(offset)], flip(me_s, distance), me_h,
            ).start()

    def head_rows(g):
        return w_buf[pl.ds(2 * g, 2)].reshape(HDIM, 2 * width)

    def own_or_other(sems, z):
        return sems.at[jnp.where(z == pair, 1, 0)]

    def g_copies(i):
        g = exclusive(2 * i, pair)
        arrived(near_buf.at[i], near_recv.at[i])
        gpart[g] += near_buf[i]

        def one(t):
            send(
                gpart.at[g, t], g_buf.at[i, to_slot(t)], own_or_other(g_send, g),
                g_recv.at[0], to_seq(t), 2 * g + side,
            )

        loop(seqs, one)

    def partial_grad(k):
        g = exclusive(k, pair)
        for offset in fresh:
            w_arrived(g, offset)
        w_high, w_low = halves(head_rows(g))
        total = jnp.zeros((rows, HDIM), jnp.float32)
        for c in range(2):
            cols = slice(c * width, (c + 1) * width)
            out = gout_buf[c]
            total = total + (
                bf16_dot(out, w_high[:, cols], NT) + bf16_dot(out, w_low[:, cols], NT)
            )
        for a in range(RUNS):
            gpart[g, :, a] = total[a * STRIDE : (a + 1) * STRIDE].reshape(seqs, res, HDIM)

        @pl.when(lax.rem(k, 2) == 1)
        def _():
            i = lax.div(k, 2)
            remote(
                gpart.at[g], near_buf.at[i], near_send.at[0], near_recv.at[i],
                me_s, 2 * neighbour + side,
            ).start()

    def w_step(step):
        for at in range(len(stages) + 1):
            turn_of = step - at - at // len(stages)

            @pl.when(jnp.logical_and(turn_of >= 0, turn_of < pairs))
            def _(at=at, turn_of=turn_of):
                k = gray(turn_of)
                if at < len(stages):
                    run_stage(at, exclusive(k, pair))
                else:
                    partial_grad(k)

    ahead = 2

    loop(ahead, w_step)

    arrived(pack_buf, pack_recv.at[0])

    lane = lax.broadcasted_iota(jnp.int32, (rows, HDIM), 1) < HALF
    lane_half = lax.broadcasted_iota(jnp.int32, (rows // 2, HDIM), 1) < HALF

    def turn(x):
        return pltpu.roll(x, HALF, 1)

    qk_first = pack_buf[0, :, :RUNS].reshape(rows, HDIM)
    qk_second = pack_buf[1, :, :RUNS].reshape(rows, HDIM)
    q_buf[...] = jnp.where(lane, qk_first, turn(qk_second))
    k_buf[...] = jnp.where(lane, turn(qk_first), qk_second)
    v_first = pack_buf[0, :, RUNS].reshape(rows // 2, HDIM)
    v_second = pack_buf[1, :, RUNS].reshape(rows // 2, HDIM)
    v_buf[:, 0] = jnp.where(lane_half, v_first, turn(v_second)).reshape(seqs, res, HDIM)
    v_buf[:, 1] = jnp.where(lane_half, turn(v_first), v_second).reshape(seqs, res, HDIM)

    res_bits = res.bit_length() - 1

    def place(dim):
        index = lax.broadcasted_iota(jnp.int32, (rows, rows), dim)
        run = (index >> res_bits) & 1
        part = index >> (res_bits + 1)
        residue = index & (res - 1)
        return run, part, residue

    run_i, part_i, residue_i = place(0)
    run_j, part_j, residue_j = place(1)
    at_i = run_i * STRIDE + part_i * res + residue_i
    at_j = run_j * STRIDE + part_j * res + residue_j
    local_ok = jnp.where((at_j <= at_i) & (run_i - run_j < span_ref[pair]), 1, 0)
    order_ok = RUNS * part_j + run_j <= RUNS * part_i + run_i
    strided_ok = jnp.where((residue_i == residue_j) & order_ok, 1, 0)
    allowed = local_ok * (1 - side) + strided_ok * side > 0

    scale = HDIM ** (-0.5)
    scores = exact_dot(q_buf[...], k_buf[...], NT) * scale
    row_max = jnp.max(jnp.where(allowed, scores, -jnp.inf), axis=-1, keepdims=True)
    weights = jnp.where(allowed, jnp.exp(scores - row_max), 0.0)
    probs = weights / jnp.sum(weights, axis=-1, keepdims=True)
    p_buf[...] = probs
    w_step(ahead)
    attended = exact_dot(probs, v_buf[...].reshape(rows, HDIM), NN)
    attn_own[...] = attended.reshape(seqs, RUNS, res, HDIM)

    def attn_copies(i):
        z = exclusive(2 * i, pair)

        def one(t):
            send(
                attn_own.at[t], attn_buf.at[pair, to_slot(t)], own_or_other(attn_send, z),
                attn_recv.at[pair], to_seq(t), 2 * z + side,
            )

        loop(seqs, one)

    loop(pairs // 2, attn_copies)

    own_inputs[3].wait()
    gout_copy.wait_recv()

    def rest(step):
        w_step(step + ahead + 1)

    loop(pairs + len(stages) - ahead, rest)

    def hand_on(i):
        g = exclusive(2 * i, pair)
        arrived(attn_buf.at[g], attn_recv.at[g])
        remote(
            attn_buf.at[g], attn_buf.at[g], hand_send.at[0], attn_recv.at[g],
            me_s, 2 * neighbour + side,
        ).start()

    loop(pairs // 2, hand_on)
    loop(pairs // 2, g_copies)

    m_buf[...] = jnp.zeros_like(m_buf)

    def partial_mixed(step):
        handed = lax.div(2 * step, pairs)
        k = 2 * (step - handed * (pairs // 2)) + handed
        g = exclusive(k, pair)

        @pl.when(handed == 1)
        def _():
            arrived(attn_buf.at[g], attn_recv.at[g])

        attn = jnp.concatenate(
            [attn_buf[g, :, a].reshape(STRIDE, HDIM) for a in range(RUNS)], axis=0
        )
        a_high, a_low = halves(attn)
        w_high, w_low = halves(head_rows(g))
        for c in range(2):
            cols = slice(c * width, (c + 1) * width)
            m_buf[c] += bf16_dot(a_high, w_high[:, cols], NN) + (
                bf16_dot(a_high, w_low[:, cols], NN) + bf16_dot(a_low, w_high[:, cols], NN)
            )

    loop(pairs, partial_mixed)
    m_copy = remote(
        m_buf.at[1 - side], m_recv, m_send.at[0], m_recv_sem.at[0], me_s, partner
    )
    m_copy.start()

    arrived(g_buf, g_recv.at[0])
    incoming = jnp.sum(g_buf[...], axis=0).reshape(rows, HDIM)
    delta = jnp.sum(incoming * attn_own[...].reshape(rows, HDIM), axis=-1, keepdims=True)
    dprobs = exact_dot(incoming, v_buf[...].reshape(rows, HDIM), NT)
    probs = p_buf[...]
    dscores = probs * (dprobs - delta)
    dq = split_dot(dscores, k_buf[...], NN) * scale
    dk = split_dot(dscores, q_buf[...], TN) * scale
    dv = split_dot(probs, incoming, TN).reshape(seqs, RUNS, res, HDIM)
    e_out[0, :, :RUNS] = jnp.where(lane, dq, turn(dk)).reshape(seqs, RUNS, res, HDIM)
    e_out[1, :, :RUNS] = jnp.where(lane, turn(dq), dk).reshape(seqs, RUNS, res, HDIM)
    dv_first = dv[:, 0].reshape(rows // 2, HDIM)
    dv_second = dv[:, 1].reshape(rows // 2, HDIM)
    e_out[0, :, RUNS] = jnp.where(lane_half, dv_first, turn(dv_second)).reshape(seqs, res, HDIM)
    e_out[1, :, RUNS] = jnp.where(lane_half, turn(dv_first), dv_second).reshape(seqs, res, HDIM)

    def e_copies(t):
        for c in range(2):
            send(
                e_out.at[c, t], e_buf.at[side, to_slot(t)], e_send.at[c],
                e_recv.at[0], to_seq(t), 2 * pair + c,
            )

    loop(seqs, e_copies)

    arrived(pack_ref, pack_send.at[1 - side])
    arrived(w_buf.at[pl.ds(0, heads - 1), 0], w_send.at[0])
    gout_copy.wait_send()
    for at, (_, held_here, _) in enumerate(stages):
        arrived(w_buf.at[:, pl.ds(0, len(held_here))], share_send.at[at])
    arrived(attn_buf.at[pl.ds(0, pairs // 2 - 1)], attn_send.at[0])
    arrived(attn_buf.at[pl.ds(0, pairs // 2)], hand_send.at[0])
    arrived(near_buf, near_send.at[0])
    arrived(gpart.at[pl.ds(0, pairs // 2 - 1)], g_send.at[0])

    @pl.when(side == 1)
    def _():
        arrived(pack_ref.at[pl.ds(0, seqs - 1)], pack_send.at[1])
        arrived(attn_own.at[pl.ds(0, seqs - 1)], attn_send.at[1])
        arrived(attn_own.at[pl.ds(0, seqs - 1)], g_send.at[1])

    m_copy.wait_recv()
    mixed_ref[...] = m_buf[side] + m_recv[...]

    arrived(e_buf, e_recv.at[0])
    grads = e_buf[0] + e_buf[1]
    query_key = jnp.concatenate([grads[:, a].reshape(STRIDE, HDIM) for a in range(RUNS)], axis=0).T
    grad_query_ref[...] = query_key[:HALF]
    grad_key_ref[...] = query_key[HALF:]
    value_pair = grads[:, RUNS].reshape(STRIDE, HDIM).T
    grad_value_ref[:, :STRIDE] = value_pair[:HALF]
    grad_value_ref[:, STRIDE:] = value_pair[HALF:]

    m_copy.wait_send()
    arrived(e_out.at[0], e_send.at[1 - side])

    @pl.when(side == 1)
    def _():
        arrived(e_out.at[0, pl.ds(0, seqs - 1)], e_send.at[1])


def write_kernel(*refs):
    count = len(refs) // 2
    for i in range(count):
        refs[count + i][...] = refs[i][...]


def local(queries, keys, values, local_span, wo_local, wo_strided, grad_out):
    seqs, heads = lax.axis_size("seq"), lax.axis_size("head")
    rows, width = grad_out.shape
    res = STRIDE // seqs
    pairs = heads // 2
    share = min(seqs, HALF // 8)
    vmem = pl.BlockSpec(memory_space=pltpu.VMEM)
    hbm = pl.BlockSpec(memory_space=pltpu.HBM)
    dma = pltpu.SemaphoreType.DMA
    f32 = jnp.float32
    results = pl.pallas_call(
        functools.partial(kernel, seqs, heads, share),
        out_shape=(
            jax.ShapeDtypeStruct((rows, width), f32),
            jax.ShapeDtypeStruct((HALF, rows), f32),
            jax.ShapeDtypeStruct((HALF, rows), f32),
            jax.ShapeDtypeStruct((HALF, rows), f32),
        ),
        in_specs=[pl.BlockSpec(memory_space=pltpu.SMEM)] + [hbm] * 6,
        out_specs=(vmem, vmem, vmem, vmem),
        scratch_shapes=[
            pltpu.VMEM((3, HALF, rows), f32),
            pltpu.VMEM((heads, share, HALF // share, 2 * width), f32),
            pltpu.VMEM((seqs, RUNS + 1, res, HDIM), f32),
            pltpu.VMEM((2, seqs, RUNS + 1, res, HDIM), f32),
            pltpu.VMEM((2, rows, width), jnp.bfloat16),
            pltpu.VMEM((rows, HDIM), f32),
            pltpu.VMEM((rows, HDIM), f32),
            pltpu.VMEM((seqs, RUNS, res, HDIM), f32),
            pltpu.VMEM((rows, rows), f32),
            pltpu.VMEM((seqs, RUNS, res, HDIM), f32),
            pltpu.VMEM((pairs, seqs, RUNS, res, HDIM), f32),
            pltpu.VMEM((pairs, seqs, RUNS, res, HDIM), f32),
            pltpu.VMEM((pairs // 2, seqs, RUNS, res, HDIM), f32),
            pltpu.VMEM((pairs // 2, seqs, RUNS, res, HDIM), f32),
            pltpu.VMEM((2, rows, width), f32),
            pltpu.VMEM((rows, width), f32),
            pltpu.VMEM((2, seqs, RUNS + 1, res, HDIM), f32),
            pltpu.VMEM((2, seqs, RUNS + 1, res, HDIM), f32),
            dma((4,)),
            dma((1,)),
            dma((pairs, share)),
            dma((max(1, share.bit_length() - 1),)),
            dma((2,)),
            dma((1,)),
            dma((1,)),
            dma((1,)),
            dma((2,)),
            dma((pairs,)),
            dma((1,)),
            dma((1,)),
            dma((pairs // 2,)),
            dma((2,)),
            dma((1,)),
            dma((1,)),
            dma((1,)),
            dma((2,)),
            dma((1,)),
        ],
        compiler_params=pltpu.CompilerParams(
            collective_id=0, has_side_effects=True, vmem_limit_bytes=60 * 1024 * 1024
        ),
        cost_estimate=pl.CostEstimate(
            flops=2 * rows * 2 * width * HDIM * pairs * 5,
            bytes_accessed=16 * rows * width,
            transcendentals=rows * rows,
        ),
    )(local_span, queries.T, keys.T, values.T, grad_out, wo_local, wo_strided)
    mixed, grad_queries, grad_keys, grad_values = pl.pallas_call(
        write_kernel,
        out_shape=[jax.ShapeDtypeStruct(x.shape, x.dtype) for x in results],
        in_specs=[vmem] * len(results),
        out_specs=[vmem] * len(results),
        compiler_params=pltpu.CompilerParams(vmem_limit_bytes=60 * 1024 * 1024),
    )(*results)
    return (mixed, grad_queries.T, grad_keys.T, grad_values.T)


def solution(mesh):
    return jax.shard_map(
        local,
        mesh=mesh,
        in_specs=(
            P("seq", "head"),
            P("seq", "head"),
            P("seq", "head"),
            P(),
            P("head", None),
            P("head", None),
            P("seq", "head"),
        ),
        out_specs=(P("seq", "head"), P("seq", "head"), P("seq", "head"), P("seq", "head")),
        check_vma=False,
    )
```

```python
import functools

import jax
import jax.numpy as jnp
from jax import lax
from jax.experimental import pallas as pl
from jax.experimental.pallas import tpu as pltpu
from jax.sharding import PartitionSpec as P

HDIM = 128
STRIDE = 128
HALF = HDIM // 2
RUNS = 2
HIGHEST = lax.Precision.HIGHEST
NN = (((1,), (0,)), ((), ()))
NT = (((1,), (1,)), ((), ()))
TN = (((0,), (0,)), ((), ()))


def exact_dot(a, b, dims):
    return lax.dot_general(a, b, dims, precision=HIGHEST, preferred_element_type=jnp.float32)


def bf16_dot(a, b, dims):
    return lax.dot_general(a, b, dims, preferred_element_type=jnp.float32)


def halves(x):
    high = x.astype(jnp.bfloat16)
    return high, (x - high.astype(jnp.float32)).astype(jnp.bfloat16)


def split_dot(a, b, dims):
    (a_high, a_low), (b_high, b_low) = halves(a), halves(b)
    return bf16_dot(a_high, b_high, dims) + (
        bf16_dot(a_high, b_low, dims) + bf16_dot(a_low, b_high, dims)
    )


def kernel(
    seqs, heads, share,
    span_ref, query_ref, key_ref, value_ref, gout_ref, wo_local_ref, wo_strided_ref,
    mixed_ref, grad_query_ref, grad_key_ref, grad_value_ref,
    in_buf, w_buf, pack_ref, pack_buf, gout_buf, q_buf, k_buf, v_buf, p_buf, attn_own, attn_buf,
    gpart, g_buf, m_buf, m_recv, e_out, e_buf,
    in_sem, w_send, w_recv, share_send, pack_send, pack_recv, gout_send, gout_recv,
    attn_send, attn_recv, g_send, g_recv, m_send, m_recv_sem, e_send, e_recv,
):
    pairs = heads // 2
    res = STRIDE // seqs
    rows = seqs * RUNS * res
    w_rows = HALF // share
    width = gout_ref.shape[1]
    me_s = lax.axis_index("seq")
    me_h = lax.axis_index("head")
    pair = lax.div(me_h, 2)
    side = lax.rem(me_h, 2)
    partner = me_h + 1 - 2 * side
    quarter = lax.rem(me_s, share)

    def to_seq(t):
        return (1 - side) * me_s + side * t

    def to_slot(t):
        return (1 - side) * t + side * me_s

    def flip(value, distance):
        return value + distance - 2 * distance * lax.rem(lax.div(value, distance), 2)

    def exclusive(one, two):
        total, bit = one + two, 1
        while bit < pairs:
            total = total - 2 * bit * lax.rem(lax.div(one, bit), 2) * lax.rem(lax.div(two, bit), 2)
            bit *= 2
        return total

    def is_me(s, h):
        return jnp.logical_and(s == me_s, h == me_h)

    def remote(src, dst, send_sem, recv_sem, s, h):
        return pltpu.make_async_remote_copy(
            src_ref=src, dst_ref=dst, send_sem=send_sem, recv_sem=recv_sem,
            device_id=(s, h), device_id_type=pl.DeviceIdType.MESH,
        )

    def send(src, dst, send_sem, recv_sem, s, h):
        same = is_me(s, h)

        @pl.when(same)
        def _():
            pltpu.make_async_copy(src, dst, recv_sem).start()

        @pl.when(jnp.logical_not(same))
        def _():
            remote(src, dst, send_sem, recv_sem, s, h).start()

    def arrived(like, sem):
        pltpu.make_async_copy(like, like, sem).wait()

    def loop(count, body):
        def step(i, carry):
            body(i)
            return carry
        lax.fori_loop(0, count, step, 0)

    own_inputs = [
        pltpu.make_async_copy(ref, in_buf.at[i], in_sem.at[i])
        for i, ref in enumerate((query_ref, key_ref, value_ref))
    ]
    own_inputs.append(pltpu.make_async_copy(gout_ref, gout_buf.at[side], in_sem.at[3]))
    for copy in own_inputs:
        copy.start()

    barrier = pltpu.get_barrier_semaphore()

    def greet(s, h):
        pl.semaphore_signal(
            barrier, inc=1, device_id=(s, h), device_id_type=pl.DeviceIdType.MESH
        )

    loop(heads - 1, lambda i: greet(me_s, lax.rem(me_h + 1 + i, heads)))

    def greet_seq(i):
        s = lax.rem(me_s + 1 + i, seqs)
        greet(s, me_h)
        greet(s, partner)

        @pl.when(side == 1)
        def _():
            loop(pairs - 1, lambda n: greet(s, lax.rem(me_h + 2 + 2 * n, heads)))

    loop(seqs - 1, greet_seq)

    pl.semaphore_wait(
        barrier, heads - 1 + 2 * (seqs - 1) + side * (seqs - 1) * (pairs - 1)
    )

    def w_copies(step):
        z = exclusive(step, pair)
        own_rows = pl.ds(pl.multiple_of(quarter * w_rows, 8), w_rows)
        cols = pl.ds(pl.multiple_of(z * 2 * width, 128), 2 * width)
        for other, source in ((0, wo_local_ref), (1, wo_strided_ref)):
            send(
                source.at[own_rows, cols], w_buf.at[me_h, quarter], w_send.at[0],
                w_recv.at[pair, quarter], me_s, 2 * z + other,
            )

    loop(pairs, w_copies)

    for copy in own_inputs[:3]:
        copy.wait()
    query_key = in_buf[:2].reshape(HDIM, rows).T
    for a in range(RUNS):
        pack_ref[:, a] = query_key[a * STRIDE : (a + 1) * STRIDE].reshape(seqs, res, HDIM)
    value_pair = jnp.concatenate([in_buf[2, :, :STRIDE], in_buf[2, :, STRIDE:]], axis=0).T
    pack_ref[:, RUNS] = value_pair.reshape(seqs, res, HDIM)

    def pack_copies(t):
        for other in range(2):
            s = (1 - other) * me_s + other * t
            slot = (1 - other) * t + other * me_s
            send(
                pack_ref.at[t], pack_buf.at[side, slot], pack_send.at[other],
                pack_recv.at[0], s, 2 * pair + other,
            )

    loop(seqs, pack_copies)

    gout_copy = remote(
        gout_ref, gout_buf.at[side], gout_send.at[0], gout_recv.at[0], me_s, partner
    )
    gout_copy.start()

    def row_part(offset):
        q = quarter
        for bit in (1, 2, 4, 8, 16, 32):
            if offset & bit:
                q = flip(q, bit)
        return q

    def w_part(z, offset):
        return w_buf.at[pl.ds(2 * z, 2), row_part(offset)]

    def w_arrived(z, offset):
        arrived(w_part(z, offset), w_recv.at[z, row_part(offset)])

    stages, held, fresh, distance = [], [0], [0], share // 2
    while distance:
        stages.append((distance, tuple(held), tuple(fresh)))
        fresh = [offset ^ distance for offset in held]
        held = held + fresh
        distance //= 2

    def run_stage(at, z):
        distance, held_here, fresh_here = stages[at]
        for offset in held_here:
            if offset in fresh_here:
                w_arrived(z, offset)
            remote(
                w_part(z, offset), w_part(z, offset), share_send.at[at],
                w_recv.at[z, row_part(offset)], flip(me_s, distance), me_h,
            ).start()

    def head_rows(g):
        return w_buf[pl.ds(2 * g, 2)].reshape(HDIM, 2 * width)

    def own_or_other(sems, z):
        return sems.at[jnp.where(z == pair, 1, 0)]

    def g_copies(g):
        def one(t):
            send(
                gpart.at[g, t], g_buf.at[pair, to_slot(t)], own_or_other(g_send, g),
                g_recv.at[0], to_seq(t), 2 * g + side,
            )

        loop(seqs, one)

    def partial_grad(g):
        for offset in fresh:
            w_arrived(g, offset)
        w_high, w_low = halves(head_rows(g))
        total = jnp.zeros((rows, HDIM), jnp.float32)
        for c in range(2):
            cols = slice(c * width, (c + 1) * width)
            out = gout_buf[c]
            total = total + (
                bf16_dot(out, w_high[:, cols], NT) + bf16_dot(out, w_low[:, cols], NT)
            )
        for a in range(RUNS):
            gpart[g, :, a] = total[a * STRIDE : (a + 1) * STRIDE].reshape(seqs, res, HDIM)
        g_copies(g)

    def w_step(step):
        for at in range(len(stages) + 1):
            turn_of = step - at - at // len(stages)

            @pl.when(jnp.logical_and(turn_of >= 0, turn_of < pairs))
            def _(at=at, turn_of=turn_of):
                z = exclusive(turn_of, pair)
                if at < len(stages):
                    run_stage(at, z)
                else:
                    partial_grad(z)

    ahead = 2

    loop(ahead, w_step)

    arrived(pack_buf, pack_recv.at[0])

    lane = lax.broadcasted_iota(jnp.int32, (rows, HDIM), 1) < HALF
    lane_half = lax.broadcasted_iota(jnp.int32, (rows // 2, HDIM), 1) < HALF

    def turn(x):
        return pltpu.roll(x, HALF, 1)

    qk_first = pack_buf[0, :, :RUNS].reshape(rows, HDIM)
    qk_second = pack_buf[1, :, :RUNS].reshape(rows, HDIM)
    q_buf[...] = jnp.where(lane, qk_first, turn(qk_second))
    k_buf[...] = jnp.where(lane, turn(qk_first), qk_second)
    v_first = pack_buf[0, :, RUNS].reshape(rows // 2, HDIM)
    v_second = pack_buf[1, :, RUNS].reshape(rows // 2, HDIM)
    v_buf[:, 0] = jnp.where(lane_half, v_first, turn(v_second)).reshape(seqs, res, HDIM)
    v_buf[:, 1] = jnp.where(lane_half, turn(v_first), v_second).reshape(seqs, res, HDIM)

    res_bits = res.bit_length() - 1

    def place(dim):
        index = lax.broadcasted_iota(jnp.int32, (rows, rows), dim)
        run = (index >> res_bits) & 1
        part = index >> (res_bits + 1)
        residue = index & (res - 1)
        return run, part, residue

    run_i, part_i, residue_i = place(0)
    run_j, part_j, residue_j = place(1)
    at_i = run_i * STRIDE + part_i * res + residue_i
    at_j = run_j * STRIDE + part_j * res + residue_j
    local_ok = jnp.where((at_j <= at_i) & (run_i - run_j < span_ref[pair]), 1, 0)
    order_ok = RUNS * part_j + run_j <= RUNS * part_i + run_i
    strided_ok = jnp.where((residue_i == residue_j) & order_ok, 1, 0)
    allowed = local_ok * (1 - side) + strided_ok * side > 0

    scale = HDIM ** (-0.5)
    scores = exact_dot(q_buf[...], k_buf[...], NT) * scale
    row_max = jnp.max(jnp.where(allowed, scores, -jnp.inf), axis=-1, keepdims=True)
    weights = jnp.where(allowed, jnp.exp(scores - row_max), 0.0)
    probs = weights / jnp.sum(weights, axis=-1, keepdims=True)
    p_buf[...] = probs
    w_step(ahead)
    attended = exact_dot(probs, v_buf[...].reshape(rows, HDIM), NN)
    attn_own[...] = attended.reshape(seqs, RUNS, res, HDIM)

    def attn_copies(step):
        z = exclusive(step, pair)

        def one(t):
            send(
                attn_own.at[t], attn_buf.at[pair, to_slot(t)], own_or_other(attn_send, z),
                attn_recv.at[pair], to_seq(t), 2 * z + side,
            )

        loop(seqs, one)

    loop(pairs, attn_copies)

    own_inputs[3].wait()
    gout_copy.wait_recv()

    def rest(step):
        w_step(step + ahead + 1)

    loop(pairs + len(stages) - ahead, rest)

    m_buf[...] = jnp.zeros_like(m_buf)

    def partial_mixed(step):
        g = exclusive(step, pair)
        arrived(attn_buf.at[g], attn_recv.at[g])
        attn = jnp.concatenate(
            [attn_buf[g, :, a].reshape(STRIDE, HDIM) for a in range(RUNS)], axis=0
        )
        a_high, a_low = halves(attn)
        w_high, w_low = halves(head_rows(g))
        for c in range(2):
            cols = slice(c * width, (c + 1) * width)
            m_buf[c] += bf16_dot(a_high, w_high[:, cols], NN) + (
                bf16_dot(a_high, w_low[:, cols], NN) + bf16_dot(a_low, w_high[:, cols], NN)
            )

    loop(pairs, partial_mixed)
    m_copy = remote(
        m_buf.at[1 - side], m_recv, m_send.at[0], m_recv_sem.at[0], me_s, partner
    )
    m_copy.start()

    arrived(g_buf, g_recv.at[0])
    incoming = jnp.sum(g_buf[...], axis=0).reshape(rows, HDIM)
    delta = jnp.sum(incoming * attn_own[...].reshape(rows, HDIM), axis=-1, keepdims=True)
    dprobs = exact_dot(incoming, v_buf[...].reshape(rows, HDIM), NT)
    probs = p_buf[...]
    dscores = probs * (dprobs - delta)
    dq = split_dot(dscores, k_buf[...], NN) * scale
    dk = split_dot(dscores, q_buf[...], TN) * scale
    dv = split_dot(probs, incoming, TN).reshape(seqs, RUNS, res, HDIM)
    e_out[0, :, :RUNS] = jnp.where(lane, dq, turn(dk)).reshape(seqs, RUNS, res, HDIM)
    e_out[1, :, :RUNS] = jnp.where(lane, turn(dq), dk).reshape(seqs, RUNS, res, HDIM)
    dv_first = dv[:, 0].reshape(rows // 2, HDIM)
    dv_second = dv[:, 1].reshape(rows // 2, HDIM)
    e_out[0, :, RUNS] = jnp.where(lane_half, dv_first, turn(dv_second)).reshape(seqs, res, HDIM)
    e_out[1, :, RUNS] = jnp.where(lane_half, turn(dv_first), dv_second).reshape(seqs, res, HDIM)

    def e_copies(t):
        for c in range(2):
            send(
                e_out.at[c, t], e_buf.at[side, to_slot(t)], e_send.at[c],
                e_recv.at[0], to_seq(t), 2 * pair + c,
            )

    loop(seqs, e_copies)

    arrived(pack_ref, pack_send.at[1 - side])
    arrived(w_buf.at[pl.ds(0, heads - 1), 0], w_send.at[0])
    gout_copy.wait_send()
    for at, (_, held_here, _) in enumerate(stages):
        arrived(w_buf.at[:, pl.ds(0, len(held_here))], share_send.at[at])
    arrived(attn_buf.at[pl.ds(0, pairs - 1)], attn_send.at[0])
    arrived(gpart.at[pl.ds(0, pairs - 1)], g_send.at[0])

    @pl.when(side == 1)
    def _():
        arrived(pack_ref.at[pl.ds(0, seqs - 1)], pack_send.at[1])
        arrived(attn_own.at[pl.ds(0, seqs - 1)], attn_send.at[1])
        arrived(attn_own.at[pl.ds(0, seqs - 1)], g_send.at[1])

    m_copy.wait_recv()
    mixed_ref[...] = m_buf[side] + m_recv[...]

    arrived(e_buf, e_recv.at[0])
    grads = e_buf[0] + e_buf[1]
    query_key = jnp.concatenate([grads[:, a].reshape(STRIDE, HDIM) for a in range(RUNS)], axis=0).T
    grad_query_ref[...] = query_key[:HALF]
    grad_key_ref[...] = query_key[HALF:]
    value_pair = grads[:, RUNS].reshape(STRIDE, HDIM).T
    grad_value_ref[:, :STRIDE] = value_pair[:HALF]
    grad_value_ref[:, STRIDE:] = value_pair[HALF:]

    m_copy.wait_send()
    arrived(e_out.at[0], e_send.at[1 - side])

    @pl.when(side == 1)
    def _():
        arrived(e_out.at[0, pl.ds(0, seqs - 1)], e_send.at[1])


def write_kernel(*refs):
    count = len(refs) // 2
    for i in range(count):
        refs[count + i][...] = refs[i][...]


def local(queries, keys, values, local_span, wo_local, wo_strided, grad_out):
    seqs, heads = lax.axis_size("seq"), lax.axis_size("head")
    rows, width = grad_out.shape
    res = STRIDE // seqs
    pairs = heads // 2
    share = min(seqs, HALF // 8)
    vmem = pl.BlockSpec(memory_space=pltpu.VMEM)
    hbm = pl.BlockSpec(memory_space=pltpu.HBM)
    dma = pltpu.SemaphoreType.DMA
    f32 = jnp.float32
    results = pl.pallas_call(
        functools.partial(kernel, seqs, heads, share),
        out_shape=(
            jax.ShapeDtypeStruct((rows, width), f32),
            jax.ShapeDtypeStruct((HALF, rows), f32),
            jax.ShapeDtypeStruct((HALF, rows), f32),
            jax.ShapeDtypeStruct((HALF, rows), f32),
        ),
        in_specs=[pl.BlockSpec(memory_space=pltpu.SMEM)] + [hbm] * 6,
        out_specs=(vmem, vmem, vmem, vmem),
        scratch_shapes=[
            pltpu.VMEM((3, HALF, rows), f32),
            pltpu.VMEM((heads, share, HALF // share, 2 * width), f32),
            pltpu.VMEM((seqs, RUNS + 1, res, HDIM), f32),
            pltpu.VMEM((2, seqs, RUNS + 1, res, HDIM), f32),
            pltpu.VMEM((2, rows, width), jnp.bfloat16),
            pltpu.VMEM((rows, HDIM), f32),
            pltpu.VMEM((rows, HDIM), f32),
            pltpu.VMEM((seqs, RUNS, res, HDIM), f32),
            pltpu.VMEM((rows, rows), f32),
            pltpu.VMEM((seqs, RUNS, res, HDIM), f32),
            pltpu.VMEM((pairs, seqs, RUNS, res, HDIM), f32),
            pltpu.VMEM((pairs, seqs, RUNS, res, HDIM), f32),
            pltpu.VMEM((pairs, seqs, RUNS, res, HDIM), f32),
            pltpu.VMEM((2, rows, width), f32),
            pltpu.VMEM((rows, width), f32),
            pltpu.VMEM((2, seqs, RUNS + 1, res, HDIM), f32),
            pltpu.VMEM((2, seqs, RUNS + 1, res, HDIM), f32),
            dma((4,)),
            dma((1,)),
            dma((pairs, share)),
            dma((max(1, share.bit_length() - 1),)),
            dma((2,)),
            dma((1,)),
            dma((1,)),
            dma((1,)),
            dma((2,)),
            dma((pairs,)),
            dma((2,)),
            dma((1,)),
            dma((1,)),
            dma((1,)),
            dma((2,)),
            dma((1,)),
        ],
        compiler_params=pltpu.CompilerParams(
            collective_id=0, has_side_effects=True, vmem_limit_bytes=60 * 1024 * 1024
        ),
        cost_estimate=pl.CostEstimate(
            flops=2 * rows * 2 * width * HDIM * pairs * 5,
            bytes_accessed=16 * rows * width,
            transcendentals=rows * rows,
        ),
    )(local_span, queries.T, keys.T, values.T, grad_out, wo_local, wo_strided)
    mixed, grad_queries, grad_keys, grad_values = pl.pallas_call(
        write_kernel,
        out_shape=[jax.ShapeDtypeStruct(x.shape, x.dtype) for x in results],
        in_specs=[vmem] * len(results),
        out_specs=[vmem] * len(results),
        compiler_params=pltpu.CompilerParams(vmem_limit_bytes=60 * 1024 * 1024),
    )(*results)
    return (mixed, grad_queries.T, grad_keys.T, grad_values.T)


def solution(mesh):
    return jax.shard_map(
        local,
        mesh=mesh,
        in_specs=(
            P("seq", "head"),
            P("seq", "head"),
            P("seq", "head"),
            P(),
            P("head", None),
            P("head", None),
            P("seq", "head"),
        ),
        out_specs=(P("seq", "head"), P("seq", "head"), P("seq", "head"), P("seq", "head")),
        check_vma=False,
    )
```

```python
import functools

import jax
import jax.numpy as jnp
from jax import lax
from jax.experimental import pallas as pl
from jax.experimental.pallas import tpu as pltpu
from jax.sharding import PartitionSpec as P

HDIM = 128
STRIDE = 128
HALF = HDIM // 2
RUNS = 2
HIGHEST = lax.Precision.HIGHEST
NN = (((1,), (0,)), ((), ()))
NT = (((1,), (1,)), ((), ()))
TN = (((0,), (0,)), ((), ()))


def exact_dot(a, b, dims):
    return lax.dot_general(a, b, dims, precision=HIGHEST, preferred_element_type=jnp.float32)


def bf16_dot(a, b, dims):
    return lax.dot_general(a, b, dims, preferred_element_type=jnp.float32)


def halves(x):
    high = x.astype(jnp.bfloat16)
    return high, (x - high.astype(jnp.float32)).astype(jnp.bfloat16)


def split_dot(a, b, dims):
    (a_high, a_low), (b_high, b_low) = halves(a), halves(b)
    return bf16_dot(a_high, b_high, dims) + (
        bf16_dot(a_high, b_low, dims) + bf16_dot(a_low, b_high, dims)
    )


def kernel(
    seqs, heads, share,
    span_ref, query_ref, key_ref, value_ref, gout_ref, wo_local_ref, wo_strided_ref,
    mixed_ref, grad_query_ref, grad_key_ref, grad_value_ref,
    in_buf, w_buf, pack_ref, pack_buf, gout_buf, q_buf, k_buf, v_buf, p_buf, attn_own, attn_buf,
    gpart, g_buf, m_buf, m_recv, e_out, e_buf,
    in_sem, w_send, w_recv, share_send, pack_send, pack_recv, gout_send, gout_recv,
    attn_send, attn_recv, g_send, g_recv, m_send, m_recv_sem, e_send, e_recv,
):
    pairs = heads // 2
    res = STRIDE // seqs
    rows = seqs * RUNS * res
    w_rows = HALF // share
    width = gout_ref.shape[1]
    me_s = lax.axis_index("seq")
    me_h = lax.axis_index("head")
    pair = lax.div(me_h, 2)
    side = lax.rem(me_h, 2)
    partner = me_h + 1 - 2 * side
    quarter = lax.rem(me_s, share)

    def to_seq(t):
        return (1 - side) * me_s + side * t

    def to_slot(t):
        return (1 - side) * t + side * me_s

    def flip(value, distance):
        return value + distance - 2 * distance * lax.rem(lax.div(value, distance), 2)

    def exclusive(one, two):
        total, bit = one + two, 1
        while bit < pairs:
            total = total - 2 * bit * lax.rem(lax.div(one, bit), 2) * lax.rem(lax.div(two, bit), 2)
            bit *= 2
        return total

    def is_me(s, h):
        return jnp.logical_and(s == me_s, h == me_h)

    def remote(src, dst, send_sem, recv_sem, s, h):
        return pltpu.make_async_remote_copy(
            src_ref=src, dst_ref=dst, send_sem=send_sem, recv_sem=recv_sem,
            device_id=(s, h), device_id_type=pl.DeviceIdType.MESH,
        )

    def send(src, dst, send_sem, recv_sem, s, h):
        same = is_me(s, h)

        @pl.when(same)
        def _():
            pltpu.make_async_copy(src, dst, recv_sem).start()

        @pl.when(jnp.logical_not(same))
        def _():
            remote(src, dst, send_sem, recv_sem, s, h).start()

    def arrived(like, sem):
        pltpu.make_async_copy(like, like, sem).wait()

    def loop(count, body):
        def step(i, carry):
            body(i)
            return carry
        lax.fori_loop(0, count, step, 0)

    own_inputs = [
        pltpu.make_async_copy(ref, in_buf.at[i], in_sem.at[i])
        for i, ref in enumerate((query_ref, key_ref, value_ref))
    ]
    own_inputs.append(pltpu.make_async_copy(gout_ref, gout_buf.at[side], in_sem.at[3]))
    for copy in own_inputs:
        copy.start()

    barrier = pltpu.get_barrier_semaphore()

    def greet(s, h):
        pl.semaphore_signal(
            barrier, inc=1, device_id=(s, h), device_id_type=pl.DeviceIdType.MESH
        )

    loop(heads - 1, lambda i: greet(me_s, lax.rem(me_h + 1 + i, heads)))

    def greet_seq(i):
        s = lax.rem(me_s + 1 + i, seqs)
        greet(s, me_h)
        greet(s, partner)

        @pl.when(side == 1)
        def _():
            loop(pairs - 1, lambda n: greet(s, lax.rem(me_h + 2 + 2 * n, heads)))

    loop(seqs - 1, greet_seq)

    pl.semaphore_wait(
        barrier, heads - 1 + 2 * (seqs - 1) + side * (seqs - 1) * (pairs - 1)
    )

    def w_copies(step):
        z = exclusive(step, pair)
        own_rows = pl.ds(pl.multiple_of(quarter * w_rows, 8), w_rows)
        cols = pl.ds(pl.multiple_of(z * 2 * width, 128), 2 * width)
        for other, source in ((0, wo_local_ref), (1, wo_strided_ref)):
            send(
                source.at[own_rows, cols], w_buf.at[me_h, quarter], w_send.at[0],
                w_recv.at[pair, quarter], me_s, 2 * z + other,
            )

    loop(pairs, w_copies)

    for copy in own_inputs[:3]:
        copy.wait()
    query_key = in_buf[:2].reshape(HDIM, rows).T
    for a in range(RUNS):
        pack_ref[:, a] = query_key[a * STRIDE : (a + 1) * STRIDE].reshape(seqs, res, HDIM)
    value_pair = jnp.concatenate([in_buf[2, :, :STRIDE], in_buf[2, :, STRIDE:]], axis=0).T
    pack_ref[:, RUNS] = value_pair.reshape(seqs, res, HDIM)

    def pack_copies(t):
        for other in range(2):
            s = (1 - other) * me_s + other * t
            slot = (1 - other) * t + other * me_s
            send(
                pack_ref.at[t], pack_buf.at[side, slot], pack_send.at[other],
                pack_recv.at[0], s, 2 * pair + other,
            )

    loop(seqs, pack_copies)

    gout_copy = remote(
        gout_ref, gout_buf.at[side], gout_send.at[0], gout_recv.at[0], me_s, partner
    )
    gout_copy.start()

    def row_part(offset):
        q = quarter
        for bit in (1, 2, 4, 8, 16, 32):
            if offset & bit:
                q = flip(q, bit)
        return q

    def w_part(z, offset):
        return w_buf.at[pl.ds(2 * z, 2), row_part(offset)]

    def w_arrived(z, offset):
        arrived(w_part(z, offset), w_recv.at[z, row_part(offset)])

    stages, held, fresh, distance = [], [0], [0], share // 2
    while distance:
        stages.append((distance, tuple(held), tuple(fresh)))
        fresh = [offset ^ distance for offset in held]
        held = held + fresh
        distance //= 2

    def run_stage(at, z):
        distance, held_here, fresh_here = stages[at]
        for offset in held_here:
            if offset in fresh_here:
                w_arrived(z, offset)
            remote(
                w_part(z, offset), w_part(z, offset), share_send.at[at],
                w_recv.at[z, row_part(offset)], flip(me_s, distance), me_h,
            ).start()

    def head_rows(g):
        return w_buf[pl.ds(2 * g, 2)].reshape(HDIM, 2 * width)

    def own_or_other(sems, z):
        return sems.at[jnp.where(z == pair, 1, 0)]

    def g_copies(g):
        def one(t):
            send(
                gpart.at[g, t], g_buf.at[pair, to_slot(t)], own_or_other(g_send, g),
                g_recv.at[0], to_seq(t), 2 * g + side,
            )

        loop(seqs, one)

    def partial_grad(g):
        for offset in fresh:
            w_arrived(g, offset)
        w_both = jnp.concatenate(halves(head_rows(g)), axis=0)
        total = bf16_dot(gout_buf[0], w_both[:, :width], NT)
        total = total + bf16_dot(gout_buf[1], w_both[:, width:], NT)
        total = total[:, :HDIM] + total[:, HDIM:]
        for a in range(RUNS):
            gpart[g, :, a] = total[a * STRIDE : (a + 1) * STRIDE].reshape(seqs, res, HDIM)
        g_copies(g)

    def w_step(step):
        for at in range(len(stages) + 1):
            turn_of = step - at - at // len(stages)

            @pl.when(jnp.logical_and(turn_of >= 0, turn_of < pairs))
            def _(at=at, turn_of=turn_of):
                z = exclusive(turn_of, pair)
                if at < len(stages):
                    run_stage(at, z)
                else:
                    partial_grad(z)

    ahead = 2

    loop(ahead, w_step)

    arrived(pack_buf, pack_recv.at[0])

    lane = lax.broadcasted_iota(jnp.int32, (rows, HDIM), 1) < HALF
    lane_half = lax.broadcasted_iota(jnp.int32, (rows // 2, HDIM), 1) < HALF

    def turn(x):
        return pltpu.roll(x, HALF, 1)

    qk_first = pack_buf[0, :, :RUNS].reshape(rows, HDIM)
    qk_second = pack_buf[1, :, :RUNS].reshape(rows, HDIM)
    q_buf[...] = jnp.where(lane, qk_first, turn(qk_second))
    k_buf[...] = jnp.where(lane, turn(qk_first), qk_second)
    v_first = pack_buf[0, :, RUNS].reshape(rows // 2, HDIM)
    v_second = pack_buf[1, :, RUNS].reshape(rows // 2, HDIM)
    v_buf[:, 0] = jnp.where(lane_half, v_first, turn(v_second)).reshape(seqs, res, HDIM)
    v_buf[:, 1] = jnp.where(lane_half, turn(v_first), v_second).reshape(seqs, res, HDIM)

    res_bits = res.bit_length() - 1

    def place(dim):
        index = lax.broadcasted_iota(jnp.int32, (rows, rows), dim)
        run = (index >> res_bits) & 1
        part = index >> (res_bits + 1)
        residue = index & (res - 1)
        return run, part, residue

    run_i, part_i, residue_i = place(0)
    run_j, part_j, residue_j = place(1)
    at_i = run_i * STRIDE + part_i * res + residue_i
    at_j = run_j * STRIDE + part_j * res + residue_j
    local_ok = jnp.where((at_j <= at_i) & (run_i - run_j < span_ref[pair]), 1, 0)
    order_ok = RUNS * part_j + run_j <= RUNS * part_i + run_i
    strided_ok = jnp.where((residue_i == residue_j) & order_ok, 1, 0)
    allowed = local_ok * (1 - side) + strided_ok * side > 0

    scale = HDIM ** (-0.5)
    scores = exact_dot(q_buf[...], k_buf[...], NT) * scale
    row_max = jnp.max(jnp.where(allowed, scores, -jnp.inf), axis=-1, keepdims=True)
    weights = jnp.where(allowed, jnp.exp(scores - row_max), 0.0)
    probs = weights / jnp.sum(weights, axis=-1, keepdims=True)
    p_buf[...] = probs
    w_step(ahead)
    attended = exact_dot(probs, v_buf[...].reshape(rows, HDIM), NN)
    attn_own[...] = attended.reshape(seqs, RUNS, res, HDIM)

    def attn_copies(step):
        z = exclusive(step, pair)

        def one(t):
            send(
                attn_own.at[t], attn_buf.at[pair, to_slot(t)], own_or_other(attn_send, z),
                attn_recv.at[pair], to_seq(t), 2 * z + side,
            )

        loop(seqs, one)

    loop(pairs, attn_copies)

    own_inputs[3].wait()
    gout_copy.wait_recv()

    def rest(step):
        w_step(step + ahead + 1)

    loop(pairs + len(stages) - ahead, rest)

    def partial_mixed(half, at, wait):
        def body(i):
            attn_parts, w_parts = [], []
            for n in range(2):
                g = exclusive(2 * i + n, pair)
                if wait:
                    arrived(attn_buf.at[g], attn_recv.at[g])
                attn = jnp.concatenate(
                    [attn_buf[g, :, a].reshape(STRIDE, HDIM) for a in range(RUNS)], axis=0
                )
                both = head_rows(g)
                a_high, a_low = halves(attn)
                w_high, w_low = halves(jnp.where(half == 0, both[:, :width], both[:, width:]))
                attn_parts += [a_high, a_low, a_high]
                w_parts += [w_high, w_high, w_low]
            m_buf[at] += bf16_dot(
                jnp.concatenate(attn_parts, axis=1), jnp.concatenate(w_parts, axis=0), NN
            )

        m_buf[at] = jnp.zeros((rows, width), jnp.float32)
        loop(pairs // 2, body)

    partial_mixed(1 - side, 0, True)
    m_copy = remote(m_buf.at[0], m_recv, m_send.at[0], m_recv_sem.at[0], me_s, partner)
    m_copy.start()

    arrived(g_buf, g_recv.at[0])
    incoming = jnp.sum(g_buf[...], axis=0).reshape(rows, HDIM)
    delta = jnp.sum(incoming * attn_own[...].reshape(rows, HDIM), axis=-1, keepdims=True)
    dprobs = exact_dot(incoming, v_buf[...].reshape(rows, HDIM), NT)
    probs = p_buf[...]
    dscores = probs * (dprobs - delta)
    dq = split_dot(dscores, k_buf[...], NN) * scale
    dk = split_dot(dscores, q_buf[...], TN) * scale
    dv = split_dot(probs, incoming, TN).reshape(seqs, RUNS, res, HDIM)
    e_out[0, :, :RUNS] = jnp.where(lane, dq, turn(dk)).reshape(seqs, RUNS, res, HDIM)
    e_out[1, :, :RUNS] = jnp.where(lane, turn(dq), dk).reshape(seqs, RUNS, res, HDIM)
    dv_first = dv[:, 0].reshape(rows // 2, HDIM)
    dv_second = dv[:, 1].reshape(rows // 2, HDIM)
    e_out[0, :, RUNS] = jnp.where(lane_half, dv_first, turn(dv_second)).reshape(seqs, res, HDIM)
    e_out[1, :, RUNS] = jnp.where(lane_half, turn(dv_first), dv_second).reshape(seqs, res, HDIM)

    def e_copies(t):
        for c in range(2):
            send(
                e_out.at[c, t], e_buf.at[side, to_slot(t)], e_send.at[c],
                e_recv.at[0], to_seq(t), 2 * pair + c,
            )

    loop(seqs, e_copies)

    partial_mixed(side, 1, False)

    arrived(pack_ref, pack_send.at[1 - side])
    arrived(w_buf.at[pl.ds(0, heads - 1), 0], w_send.at[0])
    gout_copy.wait_send()
    for at, (_, held_here, _) in enumerate(stages):
        arrived(w_buf.at[:, pl.ds(0, len(held_here))], share_send.at[at])
    arrived(attn_buf.at[pl.ds(0, pairs - 1)], attn_send.at[0])
    arrived(gpart.at[pl.ds(0, pairs - 1)], g_send.at[0])

    @pl.when(side == 1)
    def _():
        arrived(pack_ref.at[pl.ds(0, seqs - 1)], pack_send.at[1])
        arrived(attn_own.at[pl.ds(0, seqs - 1)], attn_send.at[1])
        arrived(attn_own.at[pl.ds(0, seqs - 1)], g_send.at[1])

    m_copy.wait_recv()
    mixed_ref[...] = m_buf[1] + m_recv[...]

    arrived(e_buf, e_recv.at[0])
    grads = e_buf[0] + e_buf[1]
    query_key = jnp.concatenate([grads[:, a].reshape(STRIDE, HDIM) for a in range(RUNS)], axis=0).T
    grad_query_ref[...] = query_key[:HALF]
    grad_key_ref[...] = query_key[HALF:]
    value_pair = grads[:, RUNS].reshape(STRIDE, HDIM).T
    grad_value_ref[:, :STRIDE] = value_pair[:HALF]
    grad_value_ref[:, STRIDE:] = value_pair[HALF:]

    m_copy.wait_send()
    arrived(e_out.at[0], e_send.at[1 - side])

    @pl.when(side == 1)
    def _():
        arrived(e_out.at[0, pl.ds(0, seqs - 1)], e_send.at[1])


def write_kernel(*refs):
    count = len(refs) // 2
    for i in range(count):
        refs[count + i][...] = refs[i][...]


def local(queries, keys, values, local_span, wo_local, wo_strided, grad_out):
    seqs, heads = lax.axis_size("seq"), lax.axis_size("head")
    rows, width = grad_out.shape
    res = STRIDE // seqs
    pairs = heads // 2
    share = min(seqs, HALF // 8)
    vmem = pl.BlockSpec(memory_space=pltpu.VMEM)
    hbm = pl.BlockSpec(memory_space=pltpu.HBM)
    dma = pltpu.SemaphoreType.DMA
    f32 = jnp.float32
    results = pl.pallas_call(
        functools.partial(kernel, seqs, heads, share),
        out_shape=(
            jax.ShapeDtypeStruct((rows, width), f32),
            jax.ShapeDtypeStruct((HALF, rows), f32),
            jax.ShapeDtypeStruct((HALF, rows), f32),
            jax.ShapeDtypeStruct((HALF, rows), f32),
        ),
        in_specs=[pl.BlockSpec(memory_space=pltpu.SMEM)] + [hbm] * 6,
        out_specs=(vmem, vmem, vmem, vmem),
        scratch_shapes=[
            pltpu.VMEM((3, HALF, rows), f32),
            pltpu.VMEM((heads, share, HALF // share, 2 * width), f32),
            pltpu.VMEM((seqs, RUNS + 1, res, HDIM), f32),
            pltpu.VMEM((2, seqs, RUNS + 1, res, HDIM), f32),
            pltpu.VMEM((2, rows, width), jnp.bfloat16),
            pltpu.VMEM((rows, HDIM), f32),
            pltpu.VMEM((rows, HDIM), f32),
            pltpu.VMEM((seqs, RUNS, res, HDIM), f32),
            pltpu.VMEM((rows, rows), f32),
            pltpu.VMEM((seqs, RUNS, res, HDIM), f32),
            pltpu.VMEM((pairs, seqs, RUNS, res, HDIM), f32),
            pltpu.VMEM((pairs, seqs, RUNS, res, HDIM), f32),
            pltpu.VMEM((pairs, seqs, RUNS, res, HDIM), f32),
            pltpu.VMEM((2, rows, width), f32),
            pltpu.VMEM((rows, width), f32),
            pltpu.VMEM((2, seqs, RUNS + 1, res, HDIM), f32),
            pltpu.VMEM((2, seqs, RUNS + 1, res, HDIM), f32),
            dma((4,)),
            dma((1,)),
            dma((pairs, share)),
            dma((max(1, share.bit_length() - 1),)),
            dma((2,)),
            dma((1,)),
            dma((1,)),
            dma((1,)),
            dma((2,)),
            dma((pairs,)),
            dma((2,)),
            dma((1,)),
            dma((1,)),
            dma((1,)),
            dma((2,)),
            dma((1,)),
        ],
        compiler_params=pltpu.CompilerParams(
            collective_id=0, has_side_effects=True, vmem_limit_bytes=60 * 1024 * 1024
        ),
        cost_estimate=pl.CostEstimate(
            flops=2 * rows * 2 * width * HDIM * pairs * 5,
            bytes_accessed=16 * rows * width,
            transcendentals=rows * rows,
        ),
    )(local_span, queries.T, keys.T, values.T, grad_out, wo_local, wo_strided)
    mixed, grad_queries, grad_keys, grad_values = pl.pallas_call(
        write_kernel,
        out_shape=[jax.ShapeDtypeStruct(x.shape, x.dtype) for x in results],
        in_specs=[vmem] * len(results),
        out_specs=[vmem] * len(results),
        compiler_params=pltpu.CompilerParams(vmem_limit_bytes=60 * 1024 * 1024),
    )(*results)
    return (mixed, grad_queries.T, grad_keys.T, grad_values.T)


def solution(mesh):
    return jax.shard_map(
        local,
        mesh=mesh,
        in_specs=(
            P("seq", "head"),
            P("seq", "head"),
            P("seq", "head"),
            P(),
            P("head", None),
            P("head", None),
            P("seq", "head"),
        ),
        out_specs=(P("seq", "head"), P("seq", "head"), P("seq", "head"), P("seq", "head")),
        check_vma=False,
    )
```

```python
import functools

import jax
import jax.numpy as jnp
from jax import lax
from jax.experimental import pallas as pl
from jax.experimental.pallas import tpu as pltpu
from jax.sharding import PartitionSpec as P

HDIM = 128
STRIDE = 128
HALF = HDIM // 2
RUNS = 2
HIGHEST = lax.Precision.HIGHEST
NN = (((1,), (0,)), ((), ()))
NT = (((1,), (1,)), ((), ()))
TN = (((0,), (0,)), ((), ()))


def exact_dot(a, b, dims):
    return lax.dot_general(a, b, dims, precision=HIGHEST, preferred_element_type=jnp.float32)


def bf16_dot(a, b, dims):
    return lax.dot_general(a, b, dims, preferred_element_type=jnp.float32)


def halves(x):
    high = x.astype(jnp.bfloat16)
    return high, (x - high.astype(jnp.float32)).astype(jnp.bfloat16)


def split_dot(a, b, dims):
    (a_high, a_low), (b_high, b_low) = halves(a), halves(b)
    return bf16_dot(a_high, b_high, dims) + (
        bf16_dot(a_high, b_low, dims) + bf16_dot(a_low, b_high, dims)
    )


def kernel(
    seqs, heads, share,
    span_ref, query_ref, key_ref, value_ref, gout_ref, wo_local_ref, wo_strided_ref,
    mixed_ref, grad_query_ref, grad_key_ref, grad_value_ref,
    in_buf, w_buf, pack_ref, pack_buf, gout_buf, q_buf, k_buf, v_buf, p_buf, attn_own, attn_buf,
    gpart, g_buf, m_buf, m_recv, e_out, e_buf,
    in_sem, w_send, w_recv, share_send, pack_send, pack_recv, gout_send, gout_recv,
    attn_send, attn_recv, g_send, g_recv, m_send, m_recv_sem, e_send, e_recv,
):
    pairs = heads // 2
    res = STRIDE // seqs
    rows = seqs * RUNS * res
    w_rows = HALF // share
    width = gout_ref.shape[1]
    me_s = lax.axis_index("seq")
    me_h = lax.axis_index("head")
    pair = lax.div(me_h, 2)
    side = lax.rem(me_h, 2)
    partner = me_h + 1 - 2 * side
    quarter = lax.rem(me_s, share)

    def to_seq(t):
        return (1 - side) * me_s + side * t

    def to_slot(t):
        return (1 - side) * t + side * me_s

    def flip(value, distance):
        return value + distance - 2 * distance * lax.rem(lax.div(value, distance), 2)

    def exclusive(one, two):
        total, bit = one + two, 1
        while bit < pairs:
            total = total - 2 * bit * lax.rem(lax.div(one, bit), 2) * lax.rem(lax.div(two, bit), 2)
            bit *= 2
        return total

    def is_me(s, h):
        return jnp.logical_and(s == me_s, h == me_h)

    def remote(src, dst, send_sem, recv_sem, s, h):
        return pltpu.make_async_remote_copy(
            src_ref=src, dst_ref=dst, send_sem=send_sem, recv_sem=recv_sem,
            device_id=(s, h), device_id_type=pl.DeviceIdType.MESH,
        )

    def send(src, dst, send_sem, recv_sem, s, h):
        same = is_me(s, h)

        @pl.when(same)
        def _():
            pltpu.make_async_copy(src, dst, recv_sem).start()

        @pl.when(jnp.logical_not(same))
        def _():
            remote(src, dst, send_sem, recv_sem, s, h).start()

    def arrived(like, sem):
        pltpu.make_async_copy(like, like, sem).wait()

    def loop(count, body):
        def step(i, carry):
            body(i)
            return carry
        lax.fori_loop(0, count, step, 0)

    own_inputs = [
        pltpu.make_async_copy(ref, in_buf.at[i], in_sem.at[i])
        for i, ref in enumerate((query_ref, key_ref, value_ref))
    ]
    own_inputs.append(pltpu.make_async_copy(gout_ref, gout_buf.at[side], in_sem.at[3]))
    for copy in own_inputs:
        copy.start()

    barrier = pltpu.get_barrier_semaphore()

    def greet(s, h):
        pl.semaphore_signal(
            barrier, inc=1, device_id=(s, h), device_id_type=pl.DeviceIdType.MESH
        )

    loop(heads - 1, lambda i: greet(me_s, lax.rem(me_h + 1 + i, heads)))

    def greet_seq(i):
        s = lax.rem(me_s + 1 + i, seqs)
        greet(s, me_h)
        greet(s, partner)

        @pl.when(side == 1)
        def _():
            loop(pairs - 1, lambda n: greet(s, lax.rem(me_h + 2 + 2 * n, heads)))

    loop(seqs - 1, greet_seq)

    pl.semaphore_wait(
        barrier, heads - 1 + 2 * (seqs - 1) + side * (seqs - 1) * (pairs - 1)
    )

    def w_copies(step):
        z = exclusive(step, pair)
        own_rows = pl.ds(pl.multiple_of(quarter * w_rows, 8), w_rows)
        cols = pl.ds(pl.multiple_of(z * 2 * width, 128), 2 * width)
        for other, source in ((0, wo_local_ref), (1, wo_strided_ref)):
            send(
                source.at[own_rows, cols], w_buf.at[me_h, quarter], w_send.at[0],
                w_recv.at[pair, quarter], me_s, 2 * z + other,
            )

    loop(pairs, w_copies)

    for copy in own_inputs[:3]:
        copy.wait()
    query_key = in_buf[:2].reshape(HDIM, rows).T
    for a in range(RUNS):
        pack_ref[:, a] = query_key[a * STRIDE : (a + 1) * STRIDE].reshape(seqs, res, HDIM)
    value_pair = jnp.concatenate([in_buf[2, :, :STRIDE], in_buf[2, :, STRIDE:]], axis=0).T
    pack_ref[:, RUNS] = value_pair.reshape(seqs, res, HDIM)

    def pack_copies(t):
        for other in range(2):
            s = (1 - other) * me_s + other * t
            slot = (1 - other) * t + other * me_s
            send(
                pack_ref.at[t], pack_buf.at[side, slot], pack_send.at[other],
                pack_recv.at[0], s, 2 * pair + other,
            )

    loop(seqs, pack_copies)

    gout_copy = remote(
        gout_ref, gout_buf.at[side], gout_send.at[0], gout_recv.at[0], me_s, partner
    )
    gout_copy.start()

    def row_part(offset):
        q = quarter
        for bit in (1, 2, 4, 8, 16, 32):
            if offset & bit:
                q = flip(q, bit)
        return q

    def w_part(z, offset):
        return w_buf.at[pl.ds(2 * z, 2), row_part(offset)]

    def w_arrived(z, offset):
        arrived(w_part(z, offset), w_recv.at[z, row_part(offset)])

    stages, held, fresh, distance = [], [0], [0], share // 2
    while distance:
        stages.append((distance, tuple(held), tuple(fresh)))
        fresh = [offset ^ distance for offset in held]
        held = held + fresh
        distance //= 2

    def run_stage(at, z):
        distance, held_here, fresh_here = stages[at]
        for offset in held_here:
            if offset in fresh_here:
                w_arrived(z, offset)
            remote(
                w_part(z, offset), w_part(z, offset), share_send.at[at],
                w_recv.at[z, row_part(offset)], flip(me_s, distance), me_h,
            ).start()

    def head_rows(g):
        return w_buf[pl.ds(2 * g, 2)].reshape(HDIM, 2 * width)

    def own_or_other(sems, z):
        return sems.at[jnp.where(z == pair, 1, 0)]

    def g_copies(g):
        def one(t):
            send(
                gpart.at[g, t], g_buf.at[pair, to_slot(t)], own_or_other(g_send, g),
                g_recv.at[0], to_seq(t), 2 * g + side,
            )

        loop(seqs, one)

    def partial_grad(turn_of, g):
        @pl.when(turn_of == 0)
        def _():
            own_inputs[3].wait()
            gout_copy.wait_recv()

        for offset in fresh:
            w_arrived(g, offset)
        w_both = jnp.concatenate(halves(head_rows(g)), axis=0)
        total = bf16_dot(gout_buf[0], w_both[:, :width], NT)
        total = total + bf16_dot(gout_buf[1], w_both[:, width:], NT)
        total = total[:, :HDIM] + total[:, HDIM:]
        for a in range(RUNS):
            gpart[g, :, a] = total[a * STRIDE : (a + 1) * STRIDE].reshape(seqs, res, HDIM)
        g_copies(g)

    def w_step(step):
        for at in range(len(stages) + 1):
            turn_of = step - at - at // len(stages)

            @pl.when(jnp.logical_and(turn_of >= 0, turn_of < pairs))
            def _(at=at, turn_of=turn_of):
                z = exclusive(turn_of, pair)
                if at < len(stages):
                    run_stage(at, z)
                else:
                    partial_grad(turn_of, z)

    ahead = 2

    loop(ahead, w_step)

    arrived(pack_buf, pack_recv.at[0])

    lane = lax.broadcasted_iota(jnp.int32, (rows, HDIM), 1) < HALF
    lane_half = lax.broadcasted_iota(jnp.int32, (rows // 2, HDIM), 1) < HALF

    def turn(x):
        return pltpu.roll(x, HALF, 1)

    qk_first = pack_buf[0, :, :RUNS].reshape(rows, HDIM)
    qk_second = pack_buf[1, :, :RUNS].reshape(rows, HDIM)
    q_buf[...] = jnp.where(lane, qk_first, turn(qk_second))
    k_buf[...] = jnp.where(lane, turn(qk_first), qk_second)
    v_first = pack_buf[0, :, RUNS].reshape(rows // 2, HDIM)
    v_second = pack_buf[1, :, RUNS].reshape(rows // 2, HDIM)
    v_buf[:, 0] = jnp.where(lane_half, v_first, turn(v_second)).reshape(seqs, res, HDIM)
    v_buf[:, 1] = jnp.where(lane_half, turn(v_first), v_second).reshape(seqs, res, HDIM)

    res_bits = res.bit_length() - 1

    def place(dim):
        index = lax.broadcasted_iota(jnp.int32, (rows, rows), dim)
        run = (index >> res_bits) & 1
        part = index >> (res_bits + 1)
        residue = index & (res - 1)
        return run, part, residue

    run_i, part_i, residue_i = place(0)
    run_j, part_j, residue_j = place(1)
    at_i = run_i * STRIDE + part_i * res + residue_i
    at_j = run_j * STRIDE + part_j * res + residue_j
    local_ok = jnp.where((at_j <= at_i) & (run_i - run_j < span_ref[pair]), 1, 0)
    order_ok = RUNS * part_j + run_j <= RUNS * part_i + run_i
    strided_ok = jnp.where((residue_i == residue_j) & order_ok, 1, 0)
    allowed = local_ok * (1 - side) + strided_ok * side > 0

    scale = HDIM ** (-0.5)
    scores = exact_dot(q_buf[...], k_buf[...], NT) * scale
    row_max = jnp.max(jnp.where(allowed, scores, -jnp.inf), axis=-1, keepdims=True)
    weights = jnp.where(allowed, jnp.exp(scores - row_max), 0.0)
    probs = weights / jnp.sum(weights, axis=-1, keepdims=True)
    p_buf[...] = probs
    w_step(ahead)
    attended = exact_dot(probs, v_buf[...].reshape(rows, HDIM), NN)
    attn_own[...] = attended.reshape(seqs, RUNS, res, HDIM)

    def attn_copies(step):
        z = exclusive(step, pair)

        def one(t):
            send(
                attn_own.at[t], attn_buf.at[pair, to_slot(t)], own_or_other(attn_send, z),
                attn_recv.at[pair], to_seq(t), 2 * z + side,
            )

        loop(seqs, one)

    loop(pairs, attn_copies)

    def rest(step):
        w_step(step + ahead + 1)

    loop(pairs + len(stages) - ahead, rest)

    def partial_mixed(half, at, wait):
        def body(i):
            attn_parts, w_parts = [], []
            for n in range(2):
                g = exclusive(2 * i + n, pair)
                if wait:
                    arrived(attn_buf.at[g], attn_recv.at[g])
                attn = jnp.concatenate(
                    [attn_buf[g, :, a].reshape(STRIDE, HDIM) for a in range(RUNS)], axis=0
                )
                both = head_rows(g)
                a_high, a_low = halves(attn)
                w_high, w_low = halves(jnp.where(half == 0, both[:, :width], both[:, width:]))
                attn_parts += [a_high, a_low, a_high]
                w_parts += [w_high, w_high, w_low]
            m_buf[at] += bf16_dot(
                jnp.concatenate(attn_parts, axis=1), jnp.concatenate(w_parts, axis=0), NN
            )

        m_buf[at] = jnp.zeros((rows, width), jnp.float32)
        loop(pairs // 2, body)

    partial_mixed(1 - side, 0, True)
    m_copy = remote(m_buf.at[0], m_recv, m_send.at[0], m_recv_sem.at[0], me_s, partner)
    m_copy.start()

    arrived(g_buf, g_recv.at[0])
    incoming = jnp.sum(g_buf[...], axis=0).reshape(rows, HDIM)
    delta = jnp.sum(incoming * attn_own[...].reshape(rows, HDIM), axis=-1, keepdims=True)
    dprobs = exact_dot(incoming, v_buf[...].reshape(rows, HDIM), NT)
    probs = p_buf[...]
    dscores = probs * (dprobs - delta)
    dq = split_dot(dscores, k_buf[...], NN) * scale
    dk = split_dot(dscores, q_buf[...], TN) * scale
    dv = split_dot(probs, incoming, TN).reshape(seqs, RUNS, res, HDIM)
    e_out[0, :, :RUNS] = jnp.where(lane, dq, turn(dk)).reshape(seqs, RUNS, res, HDIM)
    e_out[1, :, :RUNS] = jnp.where(lane, turn(dq), dk).reshape(seqs, RUNS, res, HDIM)
    dv_first = dv[:, 0].reshape(rows // 2, HDIM)
    dv_second = dv[:, 1].reshape(rows // 2, HDIM)
    e_out[0, :, RUNS] = jnp.where(lane_half, dv_first, turn(dv_second)).reshape(seqs, res, HDIM)
    e_out[1, :, RUNS] = jnp.where(lane_half, turn(dv_first), dv_second).reshape(seqs, res, HDIM)

    def e_copies(t):
        for c in range(2):
            send(
                e_out.at[c, t], e_buf.at[side, to_slot(t)], e_send.at[c],
                e_recv.at[0], to_seq(t), 2 * pair + c,
            )

    loop(seqs, e_copies)

    partial_mixed(side, 1, False)

    arrived(pack_ref, pack_send.at[1 - side])
    arrived(w_buf.at[pl.ds(0, heads - 1), 0], w_send.at[0])
    gout_copy.wait_send()
    for at, (_, held_here, _) in enumerate(stages):
        arrived(w_buf.at[:, pl.ds(0, len(held_here))], share_send.at[at])
    arrived(attn_buf.at[pl.ds(0, pairs - 1)], attn_send.at[0])
    arrived(gpart.at[pl.ds(0, pairs - 1)], g_send.at[0])

    @pl.when(side == 1)
    def _():
        arrived(pack_ref.at[pl.ds(0, seqs - 1)], pack_send.at[1])
        arrived(attn_own.at[pl.ds(0, seqs - 1)], attn_send.at[1])
        arrived(attn_own.at[pl.ds(0, seqs - 1)], g_send.at[1])

    m_copy.wait_recv()
    mixed_ref[...] = m_buf[1] + m_recv[...]

    arrived(e_buf, e_recv.at[0])
    grads = e_buf[0] + e_buf[1]
    query_key = jnp.concatenate([grads[:, a].reshape(STRIDE, HDIM) for a in range(RUNS)], axis=0).T
    grad_query_ref[...] = query_key[:HALF]
    grad_key_ref[...] = query_key[HALF:]
    value_pair = grads[:, RUNS].reshape(STRIDE, HDIM).T
    grad_value_ref[:, :STRIDE] = value_pair[:HALF]
    grad_value_ref[:, STRIDE:] = value_pair[HALF:]

    m_copy.wait_send()
    arrived(e_out.at[0], e_send.at[1 - side])

    @pl.when(side == 1)
    def _():
        arrived(e_out.at[0, pl.ds(0, seqs - 1)], e_send.at[1])


def write_kernel(*refs):
    count = len(refs) // 2
    for i in range(count):
        refs[count + i][...] = refs[i][...]


def local(queries, keys, values, local_span, wo_local, wo_strided, grad_out):
    seqs, heads = lax.axis_size("seq"), lax.axis_size("head")
    rows, width = grad_out.shape
    res = STRIDE // seqs
    pairs = heads // 2
    share = min(seqs, HALF // 8)
    vmem = pl.BlockSpec(memory_space=pltpu.VMEM)
    hbm = pl.BlockSpec(memory_space=pltpu.HBM)
    dma = pltpu.SemaphoreType.DMA
    f32 = jnp.float32
    results = pl.pallas_call(
        functools.partial(kernel, seqs, heads, share),
        out_shape=(
            jax.ShapeDtypeStruct((rows, width), f32),
            jax.ShapeDtypeStruct((HALF, rows), f32),
            jax.ShapeDtypeStruct((HALF, rows), f32),
            jax.ShapeDtypeStruct((HALF, rows), f32),
        ),
        in_specs=[pl.BlockSpec(memory_space=pltpu.SMEM)] + [hbm] * 6,
        out_specs=(vmem, vmem, vmem, vmem),
        scratch_shapes=[
            pltpu.VMEM((3, HALF, rows), f32),
            pltpu.VMEM((heads, share, HALF // share, 2 * width), f32),
            pltpu.VMEM((seqs, RUNS + 1, res, HDIM), f32),
            pltpu.VMEM((2, seqs, RUNS + 1, res, HDIM), f32),
            pltpu.VMEM((2, rows, width), jnp.bfloat16),
            pltpu.VMEM((rows, HDIM), f32),
            pltpu.VMEM((rows, HDIM), f32),
            pltpu.VMEM((seqs, RUNS, res, HDIM), f32),
            pltpu.VMEM((rows, rows), f32),
            pltpu.VMEM((seqs, RUNS, res, HDIM), f32),
            pltpu.VMEM((pairs, seqs, RUNS, res, HDIM), f32),
            pltpu.VMEM((pairs, seqs, RUNS, res, HDIM), f32),
            pltpu.VMEM((pairs, seqs, RUNS, res, HDIM), f32),
            pltpu.VMEM((2, rows, width), f32),
            pltpu.VMEM((rows, width), f32),
            pltpu.VMEM((2, seqs, RUNS + 1, res, HDIM), f32),
            pltpu.VMEM((2, seqs, RUNS + 1, res, HDIM), f32),
            dma((4,)),
            dma((1,)),
            dma((pairs, share)),
            dma((max(1, share.bit_length() - 1),)),
            dma((2,)),
            dma((1,)),
            dma((1,)),
            dma((1,)),
            dma((2,)),
            dma((pairs,)),
            dma((2,)),
            dma((1,)),
            dma((1,)),
            dma((1,)),
            dma((2,)),
            dma((1,)),
        ],
        compiler_params=pltpu.CompilerParams(
            collective_id=0, has_side_effects=True, vmem_limit_bytes=60 * 1024 * 1024
        ),
        cost_estimate=pl.CostEstimate(
            flops=2 * rows * 2 * width * HDIM * pairs * 5,
            bytes_accessed=16 * rows * width,
            transcendentals=rows * rows,
        ),
    )(local_span, queries.T, keys.T, values.T, grad_out, wo_local, wo_strided)
    mixed, grad_queries, grad_keys, grad_values = pl.pallas_call(
        write_kernel,
        out_shape=[jax.ShapeDtypeStruct(x.shape, x.dtype) for x in results],
        in_specs=[vmem] * len(results),
        out_specs=[vmem] * len(results),
        compiler_params=pltpu.CompilerParams(vmem_limit_bytes=60 * 1024 * 1024),
    )(*results)
    return (mixed, grad_queries.T, grad_keys.T, grad_values.T)


def solution(mesh):
    return jax.shard_map(
        local,
        mesh=mesh,
        in_specs=(
            P("seq", "head"),
            P("seq", "head"),
            P("seq", "head"),
            P(),
            P("head", None),
            P("head", None),
            P("seq", "head"),
        ),
        out_specs=(P("seq", "head"), P("seq", "head"), P("seq", "head"), P("seq", "head")),
        check_vma=False,
    )
```

```python
import functools

import jax
import jax.numpy as jnp
from jax import lax
from jax.experimental import pallas as pl
from jax.experimental.pallas import tpu as pltpu
from jax.sharding import PartitionSpec as P

HDIM = 128
STRIDE = 128
HALF = HDIM // 2
RUNS = 2
HIGHEST = lax.Precision.HIGHEST
NN = (((1,), (0,)), ((), ()))
NT = (((1,), (1,)), ((), ()))
TN = (((0,), (0,)), ((), ()))


def exact_dot(a, b, dims):
    return lax.dot_general(a, b, dims, precision=HIGHEST, preferred_element_type=jnp.float32)


def bf16_dot(a, b, dims):
    return lax.dot_general(a, b, dims, preferred_element_type=jnp.float32)


def halves(x):
    high = x.astype(jnp.bfloat16)
    return high, (x - high.astype(jnp.float32)).astype(jnp.bfloat16)


def split_dot(a, b, dims):
    (a_high, a_low), (b_high, b_low) = halves(a), halves(b)
    return bf16_dot(a_high, b_high, dims) + (
        bf16_dot(a_high, b_low, dims) + bf16_dot(a_low, b_high, dims)
    )


def kernel(
    seqs, heads, share,
    span_ref, query_ref, key_ref, value_ref, gout_ref, wo_local_ref, wo_strided_ref,
    mixed_ref, grad_query_ref, grad_key_ref, grad_value_ref,
    in_buf, w_buf, pack_ref, pack_buf, gout_buf, q_buf, k_buf, v_buf, p_buf, attn_own, attn_buf,
    gpart, g_buf, m_buf, m_recv, e_out, e_buf,
    in_sem, w_send, w_recv, share_send, pack_send, pack_recv, gout_send, gout_recv,
    attn_send, attn_recv, g_send, g_recv, m_send, m_recv_sem, e_send, e_recv,
):
    pairs = heads // 2
    res = STRIDE // seqs
    rows = seqs * RUNS * res
    w_rows = HALF // share
    width = gout_ref.shape[1]
    me_s = lax.axis_index("seq")
    me_h = lax.axis_index("head")
    pair = lax.div(me_h, 2)
    side = lax.rem(me_h, 2)
    partner = me_h + 1 - 2 * side
    quarter = lax.rem(me_s, share)

    def to_seq(t):
        return (1 - side) * me_s + side * t

    def to_slot(t):
        return (1 - side) * t + side * me_s

    def flip(value, distance):
        return value + distance - 2 * distance * lax.rem(lax.div(value, distance), 2)

    def exclusive(one, two):
        total, bit = one + two, 1
        while bit < pairs:
            total = total - 2 * bit * lax.rem(lax.div(one, bit), 2) * lax.rem(lax.div(two, bit), 2)
            bit *= 2
        return total

    def is_me(s, h):
        return jnp.logical_and(s == me_s, h == me_h)

    def remote(src, dst, send_sem, recv_sem, s, h):
        return pltpu.make_async_remote_copy(
            src_ref=src, dst_ref=dst, send_sem=send_sem, recv_sem=recv_sem,
            device_id=(s, h), device_id_type=pl.DeviceIdType.MESH,
        )

    def send(src, dst, send_sem, recv_sem, s, h):
        same = is_me(s, h)

        @pl.when(same)
        def _():
            pltpu.make_async_copy(src, dst, recv_sem).start()

        @pl.when(jnp.logical_not(same))
        def _():
            remote(src, dst, send_sem, recv_sem, s, h).start()

    def arrived(like, sem):
        pltpu.make_async_copy(like, like, sem).wait()

    def loop(count, body):
        def step(i, carry):
            body(i)
            return carry
        lax.fori_loop(0, count, step, 0)

    own_inputs = [
        pltpu.make_async_copy(ref, in_buf.at[i], in_sem.at[i])
        for i, ref in enumerate((query_ref, key_ref, value_ref))
    ]
    own_inputs.append(pltpu.make_async_copy(gout_ref, gout_buf.at[side], in_sem.at[3]))
    for copy in own_inputs:
        copy.start()

    barrier = pltpu.get_barrier_semaphore()

    def greet(s, h):
        pl.semaphore_signal(
            barrier, inc=1, device_id=(s, h), device_id_type=pl.DeviceIdType.MESH
        )

    loop(heads - 1, lambda i: greet(me_s, lax.rem(me_h + 1 + i, heads)))

    def greet_seq(i):
        s = lax.rem(me_s + 1 + i, seqs)
        greet(s, me_h)
        greet(s, partner)

        @pl.when(side == 1)
        def _():
            loop(pairs - 1, lambda n: greet(s, lax.rem(me_h + 2 + 2 * n, heads)))

    loop(seqs - 1, greet_seq)

    pl.semaphore_wait(
        barrier, heads - 1 + 2 * (seqs - 1) + side * (seqs - 1) * (pairs - 1)
    )

    def w_copies(step):
        z = exclusive(step, pair)
        own_rows = pl.ds(pl.multiple_of(quarter * w_rows, 8), w_rows)
        cols = pl.ds(pl.multiple_of(z * 2 * width, 128), 2 * width)
        for other, source in ((0, wo_local_ref), (1, wo_strided_ref)):
            send(
                source.at[own_rows, cols], w_buf.at[me_h, quarter], w_send.at[0],
                w_recv.at[pair, quarter], me_s, 2 * z + other,
            )

    loop(pairs, w_copies)

    for copy in own_inputs[:3]:
        copy.wait()
    query_key = in_buf[:2].reshape(HDIM, rows).T
    for a in range(RUNS):
        pack_ref[:, a] = query_key[a * STRIDE : (a + 1) * STRIDE].reshape(seqs, res, HDIM)
    value_pair = jnp.concatenate([in_buf[2, :, :STRIDE], in_buf[2, :, STRIDE:]], axis=0).T
    pack_ref[:, RUNS] = value_pair.reshape(seqs, res, HDIM)

    def pack_copies(t):
        for other in range(2):
            s = (1 - other) * me_s + other * t
            slot = (1 - other) * t + other * me_s
            send(
                pack_ref.at[t], pack_buf.at[side, slot], pack_send.at[other],
                pack_recv.at[0], s, 2 * pair + other,
            )

    loop(seqs, pack_copies)

    gout_copy = remote(
        gout_ref, gout_buf.at[side], gout_send.at[0], gout_recv.at[0], me_s, partner
    )
    gout_copy.start()

    def row_part(offset):
        q = quarter
        for bit in (1, 2, 4, 8, 16, 32):
            if offset & bit:
                q = flip(q, bit)
        return q

    def w_part(z, offset):
        return w_buf.at[pl.ds(2 * z, 2), row_part(offset)]

    def w_arrived(z, offset):
        arrived(w_part(z, offset), w_recv.at[z, row_part(offset)])

    stages, held, fresh, distance = [], [0], [0], share // 2
    while distance:
        stages.append((distance, tuple(held), tuple(fresh)))
        fresh = [offset ^ distance for offset in held]
        held = held + fresh
        distance //= 2

    def run_stage(at, z):
        distance, held_here, fresh_here = stages[at]
        for offset in held_here:
            if offset in fresh_here:
                w_arrived(z, offset)
            remote(
                w_part(z, offset), w_part(z, offset), share_send.at[at],
                w_recv.at[z, row_part(offset)], flip(me_s, distance), me_h,
            ).start()

    def head_rows(g):
        return w_buf[pl.ds(2 * g, 2)].reshape(HDIM, 2 * width)

    def own_or_other(sems, z):
        return sems.at[jnp.where(z == pair, 1, 0)]

    def g_copies(g):
        def one(t):
            send(
                gpart.at[g, t], g_buf.at[pair, to_slot(t)], own_or_other(g_send, g),
                g_recv.at[0], to_seq(t), 2 * g + side,
            )

        loop(seqs, one)

    def partial_grad(turn_of, g):
        @pl.when(turn_of == 0)
        def _():
            own_inputs[3].wait()
            gout_copy.wait_recv()

        for offset in fresh:
            w_arrived(g, offset)
        w_both = jnp.concatenate(halves(head_rows(g)), axis=0)
        total = bf16_dot(gout_buf[0], w_both[:, :width], NT)
        total = total + bf16_dot(gout_buf[1], w_both[:, width:], NT)
        total = total[:, :HDIM] + total[:, HDIM:]
        for a in range(RUNS):
            gpart[g, :, a] = total[a * STRIDE : (a + 1) * STRIDE].reshape(seqs, res, HDIM)
        g_copies(g)

    def w_step(step):
        for at in range(len(stages) + 1):
            turn_of = step - at - at // len(stages)

            @pl.when(jnp.logical_and(turn_of >= 0, turn_of < pairs))
            def _(at=at, turn_of=turn_of):
                z = exclusive(turn_of, pair)
                if at < len(stages):
                    run_stage(at, z)
                else:
                    partial_grad(turn_of, z)

    ahead = 2

    loop(ahead, w_step)

    arrived(pack_buf, pack_recv.at[0])

    lane = lax.broadcasted_iota(jnp.int32, (rows, HDIM), 1) < HALF
    lane_half = lax.broadcasted_iota(jnp.int32, (rows // 2, HDIM), 1) < HALF

    def turn(x):
        return pltpu.roll(x, HALF, 1)

    qk_first = pack_buf[0, :, :RUNS].reshape(rows, HDIM)
    qk_second = pack_buf[1, :, :RUNS].reshape(rows, HDIM)
    q_buf[...] = jnp.where(lane, qk_first, turn(qk_second))
    k_buf[...] = jnp.where(lane, turn(qk_first), qk_second)
    v_first = pack_buf[0, :, RUNS].reshape(rows // 2, HDIM)
    v_second = pack_buf[1, :, RUNS].reshape(rows // 2, HDIM)
    v_buf[:, 0] = jnp.where(lane_half, v_first, turn(v_second)).reshape(seqs, res, HDIM)
    v_buf[:, 1] = jnp.where(lane_half, turn(v_first), v_second).reshape(seqs, res, HDIM)

    res_bits = res.bit_length() - 1

    def place(dim):
        index = lax.broadcasted_iota(jnp.int32, (rows, rows), dim)
        run = (index >> res_bits) & 1
        part = index >> (res_bits + 1)
        residue = index & (res - 1)
        return run, part, residue

    run_i, part_i, residue_i = place(0)
    run_j, part_j, residue_j = place(1)
    at_i = run_i * STRIDE + part_i * res + residue_i
    at_j = run_j * STRIDE + part_j * res + residue_j
    local_ok = jnp.where((at_j <= at_i) & (run_i - run_j < span_ref[pair]), 1, 0)
    order_ok = RUNS * part_j + run_j <= RUNS * part_i + run_i
    strided_ok = jnp.where((residue_i == residue_j) & order_ok, 1, 0)
    allowed = local_ok * (1 - side) + strided_ok * side > 0

    scale = HDIM ** (-0.5)
    scores = exact_dot(q_buf[...], k_buf[...], NT) * scale
    row_max = jnp.max(jnp.where(allowed, scores, -jnp.inf), axis=-1, keepdims=True)
    weights = jnp.where(allowed, jnp.exp(scores - row_max), 0.0)
    probs = weights / jnp.sum(weights, axis=-1, keepdims=True)
    p_buf[...] = probs
    attended = exact_dot(probs, v_buf[...].reshape(rows, HDIM), NN)
    attn_own[...] = attended.reshape(seqs, RUNS, res, HDIM)

    def attn_copies(step):
        z = exclusive(step, pair)

        def one(t):
            send(
                attn_own.at[t], attn_buf.at[pair, to_slot(t)], own_or_other(attn_send, z),
                attn_recv.at[pair], to_seq(t), 2 * z + side,
            )

        loop(seqs, one)

    loop(pairs, attn_copies)
    w_step(ahead)

    def rest(step):
        w_step(step + ahead + 1)

    loop(pairs + len(stages) - ahead, rest)

    def partial_mixed(half, at, wait):
        def body(i):
            attn_parts, w_parts = [], []
            for n in range(2):
                g = exclusive(2 * i + n, pair)
                if wait:
                    arrived(attn_buf.at[g], attn_recv.at[g])
                attn = jnp.concatenate(
                    [attn_buf[g, :, a].reshape(STRIDE, HDIM) for a in range(RUNS)], axis=0
                )
                both = head_rows(g)
                a_high, a_low = halves(attn)
                w_high, w_low = halves(jnp.where(half == 0, both[:, :width], both[:, width:]))
                attn_parts += [a_high, a_low, a_high]
                w_parts += [w_high, w_high, w_low]
            m_buf[at] += bf16_dot(
                jnp.concatenate(attn_parts, axis=1), jnp.concatenate(w_parts, axis=0), NN
            )

        m_buf[at] = jnp.zeros((rows, width), jnp.float32)
        loop(pairs // 2, body)

    partial_mixed(1 - side, 0, True)
    m_copy = remote(m_buf.at[0], m_recv, m_send.at[0], m_recv_sem.at[0], me_s, partner)
    m_copy.start()

    arrived(g_buf, g_recv.at[0])
    incoming = jnp.sum(g_buf[...], axis=0).reshape(rows, HDIM)
    delta = jnp.sum(incoming * attn_own[...].reshape(rows, HDIM), axis=-1, keepdims=True)
    dprobs = exact_dot(incoming, v_buf[...].reshape(rows, HDIM), NT)
    probs = p_buf[...]
    dscores = probs * (dprobs - delta)
    dq = split_dot(dscores, k_buf[...], NN) * scale
    dk = split_dot(dscores, q_buf[...], TN) * scale
    dv = split_dot(probs, incoming, TN).reshape(seqs, RUNS, res, HDIM)
    e_out[0, :, :RUNS] = jnp.where(lane, dq, turn(dk)).reshape(seqs, RUNS, res, HDIM)
    e_out[1, :, :RUNS] = jnp.where(lane, turn(dq), dk).reshape(seqs, RUNS, res, HDIM)
    dv_first = dv[:, 0].reshape(rows // 2, HDIM)
    dv_second = dv[:, 1].reshape(rows // 2, HDIM)
    e_out[0, :, RUNS] = jnp.where(lane_half, dv_first, turn(dv_second)).reshape(seqs, res, HDIM)
    e_out[1, :, RUNS] = jnp.where(lane_half, turn(dv_first), dv_second).reshape(seqs, res, HDIM)

    def e_copies(t):
        for c in range(2):
            send(
                e_out.at[c, t], e_buf.at[side, to_slot(t)], e_send.at[c],
                e_recv.at[0], to_seq(t), 2 * pair + c,
            )

    loop(seqs, e_copies)

    partial_mixed(side, 1, False)

    arrived(pack_ref, pack_send.at[1 - side])
    arrived(w_buf.at[pl.ds(0, heads - 1), 0], w_send.at[0])
    gout_copy.wait_send()
    for at, (_, held_here, _) in enumerate(stages):
        arrived(w_buf.at[:, pl.ds(0, len(held_here))], share_send.at[at])
    arrived(attn_buf.at[pl.ds(0, pairs - 1)], attn_send.at[0])
    arrived(gpart.at[pl.ds(0, pairs - 1)], g_send.at[0])

    @pl.when(side == 1)
    def _():
        arrived(pack_ref.at[pl.ds(0, seqs - 1)], pack_send.at[1])
        arrived(attn_own.at[pl.ds(0, seqs - 1)], attn_send.at[1])
        arrived(attn_own.at[pl.ds(0, seqs - 1)], g_send.at[1])

    m_copy.wait_recv()
    mixed_ref[...] = m_buf[1] + m_recv[...]

    arrived(e_buf, e_recv.at[0])
    grads = e_buf[0] + e_buf[1]
    query_key = jnp.concatenate([grads[:, a].reshape(STRIDE, HDIM) for a in range(RUNS)], axis=0).T
    grad_query_ref[...] = query_key[:HALF]
    grad_key_ref[...] = query_key[HALF:]
    value_pair = grads[:, RUNS].reshape(STRIDE, HDIM).T
    grad_value_ref[:, :STRIDE] = value_pair[:HALF]
    grad_value_ref[:, STRIDE:] = value_pair[HALF:]

    m_copy.wait_send()
    arrived(e_out.at[0], e_send.at[1 - side])

    @pl.when(side == 1)
    def _():
        arrived(e_out.at[0, pl.ds(0, seqs - 1)], e_send.at[1])


def write_kernel(*refs):
    count = len(refs) // 2
    for i in range(count):
        refs[count + i][...] = refs[i][...]


def local(queries, keys, values, local_span, wo_local, wo_strided, grad_out):
    seqs, heads = lax.axis_size("seq"), lax.axis_size("head")
    rows, width = grad_out.shape
    res = STRIDE // seqs
    pairs = heads // 2
    share = min(seqs, HALF // 8)
    vmem = pl.BlockSpec(memory_space=pltpu.VMEM)
    hbm = pl.BlockSpec(memory_space=pltpu.HBM)
    dma = pltpu.SemaphoreType.DMA
    f32 = jnp.float32
    results = pl.pallas_call(
        functools.partial(kernel, seqs, heads, share),
        out_shape=(
            jax.ShapeDtypeStruct((rows, width), f32),
            jax.ShapeDtypeStruct((HALF, rows), f32),
            jax.ShapeDtypeStruct((HALF, rows), f32),
            jax.ShapeDtypeStruct((HALF, rows), f32),
        ),
        in_specs=[pl.BlockSpec(memory_space=pltpu.SMEM)] + [hbm] * 6,
        out_specs=(vmem, vmem, vmem, vmem),
        scratch_shapes=[
            pltpu.VMEM((3, HALF, rows), f32),
            pltpu.VMEM((heads, share, HALF // share, 2 * width), f32),
            pltpu.VMEM((seqs, RUNS + 1, res, HDIM), f32),
            pltpu.VMEM((2, seqs, RUNS + 1, res, HDIM), f32),
            pltpu.VMEM((2, rows, width), jnp.bfloat16),
            pltpu.VMEM((rows, HDIM), f32),
            pltpu.VMEM((rows, HDIM), f32),
            pltpu.VMEM((seqs, RUNS, res, HDIM), f32),
            pltpu.VMEM((rows, rows), f32),
            pltpu.VMEM((seqs, RUNS, res, HDIM), f32),
            pltpu.VMEM((pairs, seqs, RUNS, res, HDIM), f32),
            pltpu.VMEM((pairs, seqs, RUNS, res, HDIM), f32),
            pltpu.VMEM((pairs, seqs, RUNS, res, HDIM), f32),
            pltpu.VMEM((2, rows, width), f32),
            pltpu.VMEM((rows, width), f32),
            pltpu.VMEM((2, seqs, RUNS + 1, res, HDIM), f32),
            pltpu.VMEM((2, seqs, RUNS + 1, res, HDIM), f32),
            dma((4,)),
            dma((1,)),
            dma((pairs, share)),
            dma((max(1, share.bit_length() - 1),)),
            dma((2,)),
            dma((1,)),
            dma((1,)),
            dma((1,)),
            dma((2,)),
            dma((pairs,)),
            dma((2,)),
            dma((1,)),
            dma((1,)),
            dma((1,)),
            dma((2,)),
            dma((1,)),
        ],
        compiler_params=pltpu.CompilerParams(
            collective_id=0, has_side_effects=True, vmem_limit_bytes=60 * 1024 * 1024
        ),
        cost_estimate=pl.CostEstimate(
            flops=2 * rows * 2 * width * HDIM * pairs * 5,
            bytes_accessed=16 * rows * width,
            transcendentals=rows * rows,
        ),
    )(local_span, queries.T, keys.T, values.T, grad_out, wo_local, wo_strided)
    mixed, grad_queries, grad_keys, grad_values = pl.pallas_call(
        write_kernel,
        out_shape=[jax.ShapeDtypeStruct(x.shape, x.dtype) for x in results],
        in_specs=[vmem] * len(results),
        out_specs=[vmem] * len(results),
        compiler_params=pltpu.CompilerParams(vmem_limit_bytes=60 * 1024 * 1024),
    )(*results)
    return (mixed, grad_queries.T, grad_keys.T, grad_values.T)


def solution(mesh):
    return jax.shard_map(
        local,
        mesh=mesh,
        in_specs=(
            P("seq", "head"),
            P("seq", "head"),
            P("seq", "head"),
            P(),
            P("head", None),
            P("head", None),
            P("seq", "head"),
        ),
        out_specs=(P("seq", "head"), P("seq", "head"), P("seq", "head"), P("seq", "head")),
        check_vma=False,
    )
```
